512 devices in a mesh: dp: 128 (over x, z_lo, y, core), mp: 4 (over z_hi).
Axes of the slice: x: 4, y: 8, z: 8 (z_hi: 4, z_lo: 2; z = z_hi * 2 + z_lo), core: 2. Of those that a mesh axis runs over, the one named last changes fastest.
Arguments:
- pooled: bfloat16 [32768, 1152], P('dp'), may hold values from -24 to 24
- ln_gain: float32 [1152], replicated, may hold values from 0.5 to 1.5
- w_up: bfloat16 [1152, 2560], P(None, 'mp'), may hold values from -0.1875 to 0.1875
- b_up: float32 [2560], P('mp'), may hold values from -6 to 6
- w_down: bfloat16 [2560, 1152], P('mp'), may hold values from -0.125 to 0.125
- text: bfloat16 [32768, 1152], P(('dp', 'mp')), may hold values from -0.625 to 0.625
- logit_scale: float32 [1], replicated, may hold values from 20 to 40
- logit_bias: float32 [1], replicated, may hold values from -3 to -1
Outputs:
- up_grad: float32 [1152, 2560], P('dp', 'mp')
- text_grad: float32 [32768, 1152], P(('dp', 'mp'))
- text_loss: float32 [32768], P(('dp', 'mp'))
The draws below stay inside these ranges and needn't reach their ends.
All inputs are finite; a program needn't handle non-finite values.
Results may differ from the reference program's by a relative error of at most 0.023.
Values may be sent and summed in bfloat16 or wider, within the bound.
No kernel may reach another device: no remote copies, remote signals or barrier semaphores. Data moves between devices by JAX's collectives and lax.ppermute only.
A program may use at most 64 MiB of HBM per device.

```python
import math
import jax
import jax.numpy as jnp
from jax import lax

D = 1152
FF_W = 2560
BLOCK = 256
REACH = 3
PAIRS = 32768
N_DP = 128
N_MP = 4


def raised(array, own_key, source, target, blocks, factor):
    def block_of(dim):
        return (jnp.arange(array.shape[dim]) // (array.shape[dim] // blocks)).reshape((-1,) + (1,) * (array.ndim - 1 - dim))

    one_side = jax.random.permutation(own_key, blocks)[block_of(target)]
    far = (block_of(target) + blocks // 2) % blocks
    return jnp.where((block_of(source) == one_side) | (block_of(source) == far), factor * array, array)


def block_levels(stream_key, shape, pieces, smallest, top_value):
    loudness = 1.0
    for position, blocks in pieces:
        draws = jax.random.uniform(jax.random.fold_in(jax.random.fold_in(stream_key, 6), position), (blocks,), jnp.float32, smallest / len(pieces), top_value / len(pieces))
        loudness = loudness * jnp.repeat(jnp.exp(draws), shape[position] // blocks).reshape((-1,) + (1,) * (len(shape) - 1 - position))
    return loudness


def scatter_about(key, shape, deviation, most, cuts=(), held_as=jnp.bfloat16):
    values = jax.random.normal(key, shape, jnp.float32) * deviation
    if len(cuts) > 0:
        values = block_levels(key, shape, cuts, -0.22, 0.18) * values
    return jnp.clip(values, min=-most, max=most).astype(held_as)


def noise_with(own_key, shape, scale, limit, pieces, heavy, kind=jnp.bfloat16):
    result = scale * jax.random.normal(own_key, shape, jnp.float32)
    if pieces:
        result = result * block_levels(own_key, shape, pieces, -0.22, 0.18)
    return jnp.clip(raised(result, jax.random.fold_in(own_key, 3), *heavy), -limit, limit).astype(kind)


def setup_inputs(seed: int = 0) -> dict:
    key_list = jax.random.split(jax.random.key(seed), 9)
    return {
        "pooled": noise_with(key_list[0], (PAIRS, D), 1.0, 24.0, ((0, 128),), (0, 1, 128, 5.5)),
        "ln_gain": jnp.clip(1.0 + 0.1 * jax.random.normal(key_list[1], (D,), jnp.float32), 0.5, 1.5),
        "w_up": scatter_about(key_list[2], (D, FF_W), D ** -0.5, 0.1875, ((1, 4),)),
        "b_up": scatter_about(key_list[3], (FF_W,), 1.0, 6.0, ((0, 4),), jnp.float32),
        "w_down": scatter_about(key_list[4], (FF_W, D), FF_W ** -0.5, 0.125, ((0, 4),)),
        "text": scatter_about(key_list[5], (PAIRS, D), 0.1, 0.625, ((0, 512),)),
        "logit_scale": jnp.clip(jax.random.uniform(key_list[6], (1,), jnp.float32, 20.0, 40.0), 20.0, 40.0),
        "logit_bias": jnp.clip(jax.random.uniform(key_list[7], (1,), jnp.float32, -3.0, -1.0), -3.0, -1.0),
    }


gelu_coeff = 0.044715
root_two_pi = math.sqrt(2.0 / math.pi)

def gelu_value(hidden_pre):
    inner = root_two_pi * (hidden_pre + gelu_coeff * hidden_pre * hidden_pre * hidden_pre)
    return 0.5 * hidden_pre * (1.0 + jnp.tanh(inner))

def gelu_slope(hidden_pre):
    inner = root_two_pi * (hidden_pre + gelu_coeff * hidden_pre * hidden_pre * hidden_pre)
    tanh_value = jnp.tanh(inner)
    return 0.5 * (1.0 + tanh_value) + 0.5 * hidden_pre * (1.0 - tanh_value * tanh_value) * root_two_pi * (1.0 + 3.0 * gelu_coeff * hidden_pre * hidden_pre)

def layer_norm(rows_in, ln_gain):
    values = rows_in.astype(jnp.float32)
    center = values - lax.optimization_barrier(jnp.mean(values, axis=-1, keepdims=True))
    spread = lax.optimization_barrier(jnp.mean(center * center, axis=-1, keepdims=True))
    return (center * lax.rsqrt(spread + 1e-06) * ln_gain).astype(jnp.bfloat16)

def unit_rows(rows_float):
    inverse = lax.rsqrt(lax.optimization_barrier(jnp.sum(rows_float * rows_float, axis=-1, keepdims=True)) + 1e-06)
    return (inverse, rows_float * inverse)

def head_forward(rows_in, ln_gain, w_up, b_up, w_down):
    normed = layer_norm(rows_in, ln_gain)
    hidden_pre = jnp.dot(normed, w_up, preferred_element_type=jnp.float32) + b_up
    activation = gelu_value(hidden_pre).astype(jnp.bfloat16)
    group_width = FF_W // N_MP
    embedded = rows_in.astype(jnp.float32)
    for group_index in range(N_MP):
        lower = group_index * group_width
        partial_value = jnp.dot(activation[:, lower:lower + group_width], w_down[lower:lower + group_width], preferred_element_type=jnp.float32)
        embedded = embedded + lax.optimization_barrier(partial_value.astype(jnp.bfloat16)).astype(jnp.float32)
    return (normed, hidden_pre, embedded)

def pair_terms(left_half, right_half, scale_value, bias_value, is_pair):
    logits = scale_value * jnp.dot(left_half, right_half.T, preferred_element_type=jnp.float32) + bias_value
    pair_loss = jax.nn.softplus(logits) - is_pair * logits
    coefficient = ((jax.nn.sigmoid(logits) - is_pair) * (scale_value / (2 * REACH + 1))).astype(jnp.bfloat16)
    return (coefficient, pair_loss)

def reference(pooled, ln_gain, w_up, b_up, w_down, text, logit_scale, logit_bias):
    scale_value = logit_scale[0]
    bias_value = logit_bias[0]
    window = 2 * REACH + 1
    quarter = BLOCK // N_MP
    pooled_blocks = pooled.reshape(N_DP, BLOCK, D)
    identity = jnp.eye(BLOCK, dtype=jnp.float32)
    no_match = jnp.zeros((BLOCK, BLOCK), jnp.float32)

    def forward_one(rows_in):
        normed, hidden_pre, embedded = head_forward(rows_in, ln_gain, w_up, b_up, w_down)
        inverse, image_unit = unit_rows(embedded)
        return image_unit.astype(jnp.bfloat16)
    image_half = lax.map(forward_one, pooled_blocks)
    text_inv, text_unit = unit_rows(text.astype(jnp.float32).reshape(N_DP, BLOCK, D))
    text_half = text_unit.astype(jnp.bfloat16)
    block_ids = jnp.arange(N_DP, dtype=jnp.int32)

    def image_step(up_acc, inputs):
        rows_in, block_index = inputs
        normed, hidden_pre, embedded = head_forward(rows_in, ln_gain, w_up, b_up, w_down)
        inverse, image_unit = unit_rows(embedded)
        unit_half = image_unit.astype(jnp.bfloat16)
        partial_value = jnp.zeros((N_MP, BLOCK, D), jnp.float32)
        for offset in range(-REACH, REACH + 1):
            other = ((block_index + offset) % N_DP).astype(jnp.int32)
            neighbour = lax.dynamic_index_in_dim(text_half, other, 0, keepdims=False)
            is_pair = identity if offset == 0 else no_match
            coefficient, pair_loss = pair_terms(unit_half, neighbour, scale_value, bias_value, is_pair)
            partial_value = partial_value + jnp.einsum('iqj,qjd->qid', coefficient.reshape(BLOCK, N_MP, quarter).astype(jnp.float32), neighbour.reshape(N_MP, quarter, D).astype(jnp.float32))
        grad_unit = lax.optimization_barrier(jnp.sum(lax.optimization_barrier(partial_value.astype(jnp.bfloat16)).astype(jnp.float32), axis=0))
        radial = lax.optimization_barrier(jnp.sum(image_unit * grad_unit, axis=-1, keepdims=True))
        grad_image = (inverse * (grad_unit - image_unit * radial)).astype(jnp.bfloat16)
        grad_act = jnp.dot(grad_image, w_down.T, preferred_element_type=jnp.float32)
        grad_pre = (grad_act * gelu_slope(hidden_pre)).astype(jnp.bfloat16)
        up_acc = up_acc + jnp.dot(normed.T, grad_pre, preferred_element_type=jnp.float32)
        return (up_acc, None)
    up_grad, unused = lax.scan(image_step, jnp.zeros((D, FF_W), jnp.float32), (pooled_blocks, block_ids))

    def text_step(inputs):
        own_half, own_unit, own_inv, block_index = inputs
        text_acc = jnp.zeros((BLOCK, D), jnp.float32)
        loss_acc = jnp.zeros((BLOCK,), jnp.float32)
        for offset in range(-REACH, REACH + 1):
            other = ((block_index + offset) % N_DP).astype(jnp.int32)
            image_rows = lax.dynamic_index_in_dim(image_half, other, 0, keepdims=False)
            is_pair = identity if offset == 0 else no_match
            coefficient, pair_loss = pair_terms(image_rows, own_half, scale_value, bias_value, is_pair)
            text_acc = text_acc + jnp.dot(coefficient.T, image_rows, preferred_element_type=jnp.float32)
            loss_acc = loss_acc + lax.optimization_barrier(jnp.sum(pair_loss, axis=0))
        radial = lax.optimization_barrier(jnp.sum(own_unit * text_acc, axis=-1, keepdims=True))
        grad_text = own_inv * (text_acc - own_unit * radial)
        return (grad_text, loss_acc / (window * BLOCK))
    text_grad, text_loss = lax.map(text_step, (text_half, text_unit, text_inv, block_ids))
    return (up_grad, text_grad.reshape(PAIRS, D), text_loss.reshape(PAIRS))
```

```python
import math

import jax
import jax.numpy as jnp
from jax import lax
from jax.sharding import Mesh, PartitionSpec as P

REACH = 3
WINDOW = 2 * REACH + 1
CHIPS = ("x", "zl", "y")
DP = ("x", "zl", "y", "c")
N_DP = 128

gelu_coeff = 0.044715
root_two_pi = math.sqrt(2.0 / math.pi)
f32 = jnp.float32
bf16 = jnp.bfloat16


def moved(value, pairs):
    return lax.ppermute(value, DP, [(s % N_DP, d % N_DP) for s, d in pairs])


def swapped(value):
    return lax.ppermute(value, "c", [(0, 1), (1, 0)])


def gelu_value(hidden_pre):
    inner = root_two_pi * (hidden_pre + gelu_coeff * hidden_pre * hidden_pre * hidden_pre)
    return 0.5 * hidden_pre * (1.0 + jnp.tanh(inner))


def gelu_slope(hidden_pre):
    inner = root_two_pi * (hidden_pre + gelu_coeff * hidden_pre * hidden_pre * hidden_pre)
    tanh_value = jnp.tanh(inner)
    return 0.5 * (1.0 + tanh_value) + 0.5 * hidden_pre * (
        1.0 - tanh_value * tanh_value
    ) * root_two_pi * (1.0 + 3.0 * gelu_coeff * hidden_pre * hidden_pre)


def layer_norm(rows_in, ln_gain):
    values = rows_in.astype(f32)
    center = values - jnp.mean(values, axis=-1, keepdims=True)
    spread = jnp.mean(center * center, axis=-1, keepdims=True)
    return (center * lax.rsqrt(spread + 1e-06) * ln_gain).astype(bf16)


def unit_rows(rows_float):
    inverse = lax.rsqrt(jnp.sum(rows_float * rows_float, axis=-1, keepdims=True) + 1e-06)
    return (inverse, rows_float * inverse)


def dot(a, b, ca, cb):
    return lax.dot_general(a, b, (((ca,), (cb,)), ((), ())), preferred_element_type=f32)


def mp_sum_rows(partial, quarter):
    parts = lax.all_to_all(partial.reshape(4, quarter, -1), "mp", 0, 0, tiled=True)
    return jnp.sum(parts.astype(f32), axis=0)


def body(pooled, ln_gain, w_up, b_up, w_down, text, logit_scale, logit_bias):
    rows_count, width = pooled.shape
    quarter = text.shape[0]
    units = w_up.shape[1]
    own_rows = width // N_DP
    scale_value = logit_scale[0]
    bias_value = logit_bias[0]
    core = lax.axis_index("c")
    group = lax.axis_index("mp")

    normed = layer_norm(pooled, ln_gain)
    hidden_pre = jnp.dot(normed, w_up, preferred_element_type=f32) + b_up
    activation = gelu_value(hidden_pre).astype(bf16)
    partial_out = jnp.dot(activation, w_down, preferred_element_type=f32).astype(bf16)
    summed = mp_sum_rows(partial_out, quarter)

    text_inv, text_unit = unit_rows(text.astype(f32))
    text_half = text_unit.astype(bf16)
    pair = lax.all_gather(text_half, "c", axis=0, tiled=True)
    left = moved(pair, [(i, i + 2) for i in range(N_DP)])
    right = moved(pair, [(i, i - 2) for i in range(N_DP)])
    far_out = [(i - 3, i) if i % 2 == 0 else (i + 3, i) for i in range(N_DP)]
    far = moved(text_half, far_out)
    texts = jnp.concatenate([left, pair, right, far], axis=0)

    feature = lax.broadcasted_iota(jnp.int32, (width, width // 2), 0)
    slot = lax.broadcasted_iota(jnp.int32, (width, width // 2), 1)
    wanted = (slot // own_rows) * (2 * own_rows) + slot % own_rows
    mine = (feature == wanted + core * own_rows).astype(bf16)
    theirs = (feature == wanted + (1 - core) * own_rows).astype(bf16)
    normed_mine = jnp.dot(normed, mine, preferred_element_type=f32).astype(bf16)
    normed_theirs = swapped(jnp.dot(normed, theirs, preferred_element_type=f32).astype(bf16))

    own_pooled = lax.dynamic_slice_in_dim(pooled, group * quarter, quarter, 0)
    embedded = own_pooled.astype(f32) + summed
    inverse, image_unit = unit_rows(embedded)
    unit_half = lax.all_gather(image_unit.astype(bf16), "mp", axis=0, tiled=True)

    logits = scale_value * dot(unit_half, texts, 1, 1) + bias_value
    row_ids = lax.broadcasted_iota(jnp.int32, logits.shape, 0)
    col_ids = lax.broadcasted_iota(jnp.int32, logits.shape, 1)
    own_col = col_ids - (2 + core) * quarter
    is_pair = (
        (own_col >= 0) & (own_col < quarter) & (row_ids == own_col + group * quarter)
    ).astype(f32)
    pair_loss = jax.nn.softplus(logits) - is_pair * logits
    coefficient = ((jax.nn.sigmoid(logits) - is_pair) * (scale_value / WINDOW)).astype(bf16)
    image_part = dot(coefficient, texts, 1, 0).astype(bf16)
    grad_sum = mp_sum_rows(image_part, quarter)

    radial = jnp.sum(image_unit * grad_sum, axis=-1, keepdims=True)
    grad_own = (inverse * (grad_sum - image_unit * radial)).astype(bf16)
    grad_image = lax.all_gather(grad_own, "mp", axis=0, tiled=True)
    grad_act = dot(grad_image, w_down, 1, 1)
    grad_pre = (grad_act * gelu_slope(hidden_pre)).astype(bf16)
    grad_other = swapped(grad_pre)
    up_part = dot(normed_mine, grad_pre, 0, 0) + dot(normed_theirs, grad_other, 0, 0)
    chips = N_DP // 2
    lanes = 128
    packed = own_rows * units // lanes
    up_wire = jnp.pad(
        up_part.astype(bf16).reshape(chips, packed, lanes), ((0, 0), (0, -packed % 16), (0, 0))
    )
    up_terms = lax.all_to_all(up_wire, CHIPS, 0, 0, tiled=True)
    up_grad = jnp.sum(up_terms.astype(f32), axis=0)[:packed].reshape(own_rows, units)

    text_part = dot(coefficient, unit_half, 0, 0)
    loss_part = jnp.sum(pair_loss, axis=0)
    loss_high = loss_part.astype(bf16)
    loss_low = (loss_part - loss_high.astype(f32)).astype(bf16)
    loss_cols = jnp.pad(jnp.stack([loss_high, loss_low], axis=1).astype(f32), ((0, 0), (0, lanes - 2)))
    both = jnp.concatenate([text_part, loss_cols], axis=1)
    q = quarter
    left_part, right_part, far_part = both[: 2 * q], both[4 * q : 6 * q], both[6 * q :]
    own_first, own_second = both[2 * q : 3 * q], both[3 * q : 4 * q]
    first = core == 0
    keep_side = jnp.where(first, left_part, right_part)
    give_side = jnp.where(first, right_part, left_part)
    keep_own = jnp.where(first, own_first, own_second)
    give_own = jnp.where(first, own_second, own_first)
    got = swapped(jnp.concatenate([give_side, give_own], axis=0).astype(bf16)).astype(f32)
    side = (keep_side + got[: 2 * q]).astype(bf16)
    own_sum = keep_own + got[2 * q :]
    came = moved(side, [(i, i - 2) if i % 2 == 0 else (i, i + 2) for i in range(N_DP)])
    far_back = moved(far_part.astype(bf16), [(d, s) for s, d in far_out])
    came_first, came_second = came[:q], came[q:]
    last = swapped(jnp.where(first, came_second, came_first))
    total = (
        own_sum
        + jnp.where(first, came_first, came_second).astype(f32)
        + last.astype(f32)
        + far_back.astype(f32)
    )
    text_acc = total[:, :width]
    text_loss = (total[:, width] + total[:, width + 1]) / (WINDOW * rows_count)
    text_radial = jnp.sum(text_unit * text_acc, axis=-1, keepdims=True)
    text_grad = text_inv * (text_acc - text_unit * text_radial)
    return (up_grad, text_grad, text_loss)


def solution(mesh):
    fine = Mesh(mesh.devices.reshape(4, 2, 8, 2, 4), ("x", "zl", "y", "c", "mp"))
    every = (*DP, "mp")
    placed = (
        P(DP, None),
        P(),
        P(None, "mp"),
        P("mp"),
        P("mp", None),
        P(every, None),
        P(),
        P(),
    )
    return jax.shard_map(
        body,
        mesh=fine,
        in_specs=placed,
        out_specs=(P(DP, "mp"), P(every, None), P(every)),
        check_vma=False,
    )
```

```python
import math

import jax
import jax.numpy as jnp
from jax import lax
from jax.experimental import pallas as pl
from jax.experimental.pallas import tpu as pltpu
from jax.sharding import Mesh, PartitionSpec as P

REACH = 3
WINDOW = 2 * REACH + 1
CHIPS = ("x", "zl", "y")
DP = ("x", "zl", "y", "c")
N_DP = 128
LANES = 128

gelu_coeff = 0.044715
root_two_pi = math.sqrt(2.0 / math.pi)
f32 = jnp.float32
bf16 = jnp.bfloat16
VMEM = pl.BlockSpec(memory_space=pltpu.VMEM)
SMEM = pl.BlockSpec(memory_space=pltpu.SMEM)
ANY = pl.BlockSpec(memory_space=pl.ANY)


def shape(dims, kind):
    return jax.ShapeDtypeStruct(dims, kind)


def call(kernel, outs, ins, *args, scratch=()):
    return pl.pallas_call(
        kernel,
        out_shape=outs,
        in_specs=ins,
        out_specs=jax.tree.map(lambda _: VMEM, outs),
        scratch_shapes=list(scratch),
        compiler_params=pltpu.CompilerParams(vmem_limit_bytes=40 * 1024 * 1024),
    )(*args)


def after(value, *earlier):
    return lax.optimization_barrier((value, *earlier))[0]


def moved(value, pairs):
    return lax.ppermute(value, DP, [(s % N_DP, d % N_DP) for s, d in pairs])


def swapped(value):
    return lax.ppermute(value, "c", [(0, 1), (1, 0)])


def dot(a, b, ca, cb):
    return lax.dot_general(a, b, (((ca,), (cb,)), ((), ())), preferred_element_type=f32)


def unit_rows(rows_float):
    inverse = lax.rsqrt(jnp.sum(rows_float * rows_float, axis=-1, keepdims=True) + 1e-06)
    return (inverse, rows_float * inverse)


def head_kernel(pooled, gain, b_up, w_up, w_down, normed_out, partial, slope, up, down, sems):
    copy_up = pltpu.make_async_copy(w_up, up, sems.at[0])
    copy_down = pltpu.make_async_copy(w_down, down, sems.at[1])
    copy_up.start()
    copy_down.start()
    values = pooled[...].astype(f32)
    center = values - jnp.mean(values, axis=-1, keepdims=True)
    spread = jnp.mean(center * center, axis=-1, keepdims=True)
    normed = (center * lax.rsqrt(spread + 1e-06) * gain[...]).astype(bf16)
    normed_out[...] = normed
    copy_up.wait()
    hidden = jnp.dot(normed, up[...], preferred_element_type=f32) + b_up[...]
    square = hidden * hidden
    tanh_value = jnp.tanh(root_two_pi * (hidden + gelu_coeff * square * hidden))
    half = 0.5 * (1.0 + tanh_value)
    activation = (hidden * half).astype(bf16)
    slope[...] = half + 0.5 * hidden * (1.0 - tanh_value * tanh_value) * (
        root_two_pi * (1.0 + 3.0 * gelu_coeff * square)
    )
    copy_down.wait()
    partial[...] = jnp.dot(activation, down[...], preferred_element_type=f32).astype(bf16)


def text_kernel(text, half):
    half[...] = unit_rows(text[...].astype(f32))[1].astype(bf16)


def select_kernel(info, normed, mine, theirs):
    core = info[0]
    rows = 256
    count, width = mine.shape[0], normed.shape[1]
    normed_value = normed[...]
    for out, parity in ((mine, core), (theirs, 1 - core)):
        for start in range(0, count, rows):
            row = lax.broadcasted_iota(jnp.int32, (rows, 1), 0) + start
            chip = (row % (count // 2)) // 8
            within = jnp.where(row < count // 2, row % 8, 8)
            wanted = 18 * chip + 9 * parity + within
            feature = lax.broadcasted_iota(jnp.int32, (rows, width), 1)
            pick = jnp.where(feature == wanted, 1.0, 0.0).astype(bf16)
            out[start : start + rows, :] = dot(pick, normed_value, 1, 1).astype(bf16)


def embed_kernel(info, parts, pooled, unit, half, inverse):
    quarter = parts.shape[1]
    own = pooled[pl.ds(pl.multiple_of(info[1] * quarter, quarter), quarter), :].astype(f32)
    embedded = own + (
        (parts[0].astype(f32) + parts[1].astype(f32))
        + (parts[2].astype(f32) + parts[3].astype(f32))
    )
    inv, unit_value = unit_rows(embedded)
    unit[...] = unit_value
    half[...] = unit_value.astype(bf16)
    inverse[...] = inv


def coefficients(logits, is_pair, scale):
    small = jnp.exp(-jnp.abs(logits))
    sigmoid = jnp.where(logits >= 0, 1.0, small) / (1.0 + small)
    if is_pair is not None:
        sigmoid = sigmoid - is_pair
    return (sigmoid * (scale / WINDOW)).astype(bf16), small


def image_kernel(info, factors, unit_half, left, pair, right, far, image_part):
    core, group = info[0], info[1]
    scale, bias = factors[0], factors[1]
    images = unit_half[...]
    quarter = far.shape[0]
    total = None
    for ref in (left, pair, right, far):
        texts = ref[...]
        logits = scale * dot(images, texts, 1, 1) + bias
        is_pair = None
        if ref is pair:
            row = lax.broadcasted_iota(jnp.int32, logits.shape, 0) - group * quarter
            col = lax.broadcasted_iota(jnp.int32, logits.shape, 1) - core * quarter
            is_pair = jnp.where((row == col) & (row >= 0) & (row < quarter), 1.0, 0.0)
        coefficient, _ = coefficients(logits, is_pair, scale)
        term = dot(coefficient, texts, 1, 0)
        total = term if total is None else total + term
    image_part[...] = total.astype(bf16)


def text_part_kernel(
    info, factors, unit_half, left, pair, right, far, give, far_part, keep_side, keep_own
):
    core, group = info[0], info[1]
    scale, bias = factors[0], factors[1]
    images = unit_half[...]
    quarter = far.shape[0]
    width = images.shape[1]
    first = core == 0

    def terms(ref):
        logits = scale * dot(ref[...], images, 1, 1) + bias
        is_pair = None
        if ref is pair:
            row = lax.broadcasted_iota(jnp.int32, logits.shape, 0) - core * quarter
            col = lax.broadcasted_iota(jnp.int32, logits.shape, 1) - group * quarter
            is_pair = jnp.where((row == col) & (row >= 0) & (row < quarter), 1.0, 0.0)
        coefficient, small = coefficients(logits, is_pair, scale)
        loss = jnp.maximum(logits, 0.0) + jnp.log1p(small)
        if is_pair is not None:
            loss = loss - is_pair * logits
        loss = jnp.sum(loss, axis=1, keepdims=True)
        lane = lax.broadcasted_iota(jnp.int32, (loss.shape[0], LANES), 1)
        return dot(coefficient, images, 1, 0), jnp.where(lane == 0, loss, 0.0)

    left_terms, pair_terms, right_terms, far_terms = (terms(r) for r in (left, pair, right, far))
    for k, cols in ((0, slice(0, width)), (1, slice(width, width + LANES))):
        keep_side[:, cols] = jnp.where(first, left_terms[k], right_terms[k])
        give[: 2 * quarter, cols] = jnp.where(first, right_terms[k], left_terms[k]).astype(bf16)
        one, two = pair_terms[k][:quarter], pair_terms[k][quarter:]
        keep_own[:, cols] = jnp.where(first, one, two)
        give[2 * quarter :, cols] = jnp.where(first, two, one).astype(bf16)
        far_part[:, cols] = far_terms[k].astype(bf16)


def grad_kernel(parts, unit, inverse, grad):
    grad_sum = (parts[0].astype(f32) + parts[1].astype(f32)) + (
        parts[2].astype(f32) + parts[3].astype(f32)
    )
    unit_value = unit[...]
    radial = jnp.sum(unit_value * grad_sum, axis=-1, keepdims=True)
    grad[...] = (inverse[...] * (grad_sum - unit_value * radial)).astype(bf16)


def pre_kernel(grad_image, w_down, slope, grad_pre):
    grad_act = dot(grad_image[...], w_down[...], 1, 1)
    grad_pre[...] = (grad_act * slope[...]).astype(bf16)


def up_kernel(info, mine, got, grads, wire):
    rows = grads.shape[0] // 2
    core = info[0]
    own = grads[pl.ds(pl.multiple_of(core * rows, rows), rows), :]
    other = grads[pl.ds(pl.multiple_of((1 - core) * rows, rows), rows), :]
    count = mine.shape[0] // 2
    chips = wire.shape[0]
    main = dot(mine[:count, :], own, 1, 0) + dot(got[:count, :], other, 1, 0)
    rest = dot(mine[count:, :], own, 1, 0) + dot(got[count:, :], other, 1, 0)
    place = lax.broadcasted_iota(jnp.int32, (count, LANES), 0) % 8
    blocks = [main[:, k * LANES : (k + 1) * LANES] for k in range(5)]
    ninth = jnp.zeros((count, LANES), f32)
    for k in range(5):
        ninth = jnp.where(place == k, rest[:, k * LANES : (k + 1) * LANES], ninth)
    blocks.append(ninth)
    for k in range(3):
        both = jnp.concatenate(
            [blocks[k].reshape(chips, 8, LANES), blocks[k + 3].reshape(chips, 8, LANES)], axis=1
        )
        wire[:, :, k * LANES : (k + 1) * LANES] = both.astype(bf16)


def up_sum_kernel(terms, up_grad):
    total = jnp.sum(terms[...].astype(f32), axis=0)
    up_grad[:8, : 3 * LANES] = total[:8, :]
    up_grad[:8, 3 * LANES :] = total[8:, : 2 * LANES]
    for k in range(5):
        up_grad[8:9, k * LANES : (k + 1) * LANES] = total[8 + k : 9 + k, 2 * LANES :]


def body(pooled, ln_gain, w_up, b_up, w_down, text, logit_scale, logit_bias):
    rows_count, width = pooled.shape
    q = text.shape[0]
    units = w_up.shape[1]
    core = lax.axis_index("c")
    first = core == 0
    info = jnp.stack([core, lax.axis_index("mp")]).astype(jnp.int32)
    factors = jnp.concatenate([logit_scale, logit_bias])
    wide = width + LANES

    def mp_exchange(partial):
        return lax.all_to_all(partial.reshape(4, q, width), "mp", 0, 0, tiled=True)

    normed, partial_out, slope = call(
        head_kernel,
        (
            shape((rows_count, width), bf16),
            shape((rows_count, width), bf16),
            shape((rows_count, units), f32),
        ),
        [VMEM, VMEM, VMEM, ANY, ANY],
        pooled,
        ln_gain.reshape(1, width),
        b_up.reshape(1, units),
        w_up,
        w_down,
        scratch=(
            pltpu.VMEM(w_up.shape, bf16),
            pltpu.VMEM(w_down.shape, bf16),
            pltpu.SemaphoreType.DMA((2,)),
        ),
    )
    parts = mp_exchange(partial_out)

    text_half = call(text_kernel, shape((q, width), bf16), [VMEM], after(text, partial_out))
    pair = lax.all_gather(text_half, "c", axis=0, tiled=True)
    left = moved(pair, [(i, i + 2) for i in range(N_DP)])
    right = moved(pair, [(i, i - 2) for i in range(N_DP)])
    far_out = [(i - 3, i) if i % 2 == 0 else (i + 3, i) for i in range(N_DP)]
    far = moved(text_half, far_out)
    window = (left, pair, right, far)

    half_rows = shape((1024, rows_count), bf16)
    mine, theirs = call(select_kernel, (half_rows, half_rows), [SMEM, VMEM], info, normed)
    got_rows = swapped(theirs)

    image_unit, image_half, inverse = call(
        embed_kernel,
        (shape((q, width), f32), shape((q, width), bf16), shape((q, 1), f32)),
        [SMEM, VMEM, VMEM],
        info,
        parts,
        pooled,
    )
    unit_half = lax.all_gather(image_half, "mp", axis=0, tiled=True)

    image_part = call(
        image_kernel,
        shape((rows_count, width), bf16),
        [SMEM, SMEM] + [VMEM] * 5,
        info,
        factors,
        unit_half,
        *window,
    )
    grad_parts = mp_exchange(image_part)

    give, far_part, keep_side, keep_own = call(
        text_part_kernel,
        (
            shape((3 * q, wide), bf16),
            shape((q, wide), bf16),
            shape((2 * q, wide), f32),
            shape((q, wide), f32),
        ),
        [SMEM, SMEM] + [VMEM] * 5,
        info,
        factors,
        after(unit_half, image_part),
        *window,
    )
    got = swapped(give).astype(f32)
    side = (keep_side + got[: 2 * q]).astype(bf16)
    own_sum = keep_own + got[2 * q :]
    came = moved(side, [(i, i - 2) if i % 2 == 0 else (i, i + 2) for i in range(N_DP)])
    far_back = moved(far_part, [(d, s) for s, d in far_out])

    grad_own = call(
        grad_kernel, shape((q, width), bf16), [VMEM] * 3, grad_parts, image_unit, inverse
    )
    grad_image = lax.all_gather(grad_own, "mp", axis=0, tiled=True)
    grad_pre = call(
        pre_kernel, shape((rows_count, units), bf16), [VMEM] * 3, grad_image, w_down, slope
    )
    grads = lax.all_gather(grad_pre, "c", axis=0, tiled=True)
    up_wire = call(
        up_kernel,
        shape((N_DP // 2, 16, 3 * LANES), bf16),
        [SMEM] + [VMEM] * 3,
        info,
        mine,
        got_rows,
        grads,
    )
    up_terms = lax.all_to_all(up_wire, CHIPS, 0, 0, tiled=True)

    came = after(came, up_wire)
    came_first, came_second = came[:q], came[q:]
    last = swapped(jnp.where(first, came_second, came_first))
    total = (
        own_sum
        + jnp.where(first, came_first, came_second).astype(f32)
        + last.astype(f32)
        + far_back.astype(f32)
    )
    text_acc = total[:, :width]
    text_loss = total[:, width] / (WINDOW * rows_count)
    text_inv, text_unit = unit_rows(text.astype(f32))
    text_radial = jnp.sum(text_unit * text_acc, axis=-1, keepdims=True)
    text_grad = text_inv * (text_acc - text_unit * text_radial)

    up_grad = call(up_sum_kernel, shape((width // N_DP, units), f32), [VMEM], up_terms)
    return (up_grad, text_grad, text_loss)


def solution(mesh):
    fine = Mesh(mesh.devices.reshape(4, 2, 8, 2, 4), ("x", "zl", "y", "c", "mp"))
    every = (*DP, "mp")
    placed = (
        P(DP, None),
        P(),
        P(None, "mp"),
        P("mp"),
        P("mp", None),
        P(every, None),
        P(),
        P(),
    )
    return jax.shard_map(
        body,
        mesh=fine,
        in_specs=placed,
        out_specs=(P(DP, "mp"), P(every, None), P(every)),
        check_vma=False,
    )
```

```python
import math

import jax
import jax.numpy as jnp
from jax import lax
from jax.experimental import pallas as pl
from jax.experimental.pallas import tpu as pltpu
from jax.sharding import Mesh, PartitionSpec as P

REACH = 3
WINDOW = 2 * REACH + 1
CHIPS = ("x", "zl", "y")
DP = ("x", "zl", "y", "c")
N_DP = 128
LANES = 128

gelu_coeff = 0.044715
root_two_pi = math.sqrt(2.0 / math.pi)
f32 = jnp.float32
bf16 = jnp.bfloat16
VMEM = pl.BlockSpec(memory_space=pltpu.VMEM)
SMEM = pl.BlockSpec(memory_space=pltpu.SMEM)
HBM = pl.BlockSpec(memory_space=pltpu.HBM)


def shape(dims, kind):
    return jax.ShapeDtypeStruct(dims, kind)


def call(kernel, outs, ins, *args, scratch=(), specs=None):
    return pl.pallas_call(
        kernel,
        out_shape=outs,
        in_specs=ins,
        out_specs=specs if specs is not None else jax.tree.map(lambda _: VMEM, outs),
        scratch_shapes=list(scratch),
        cost_estimate=pl.CostEstimate(flops=1, transcendentals=0, bytes_accessed=1),
        compiler_params=pltpu.CompilerParams(vmem_limit_bytes=20 * 1024 * 1024),
    )(*args)


def copied(sems, *pairs):
    copies = [pltpu.make_async_copy(a, b, sems.at[k]) for k, (a, b) in enumerate(pairs)]
    for copy in copies:
        copy.start()
    return copies


def in_hbm(value):
    return pltpu.with_memory_space_constraint(value, pltpu.HBM)


def after(value, *earlier):
    return lax.optimization_barrier((value, *earlier))[0]


def moved(value, pairs):
    return lax.ppermute(value, DP, [(s % N_DP, d % N_DP) for s, d in pairs])


def swapped(value):
    return lax.ppermute(value, "c", [(0, 1), (1, 0)])


def dot(a, b, ca, cb):
    return lax.dot_general(a, b, (((ca,), (cb,)), ((), ())), preferred_element_type=f32)


def unit_rows(rows_float):
    inverse = lax.rsqrt(jnp.sum(rows_float * rows_float, axis=-1, keepdims=True) + 1e-06)
    return (inverse, rows_float * inverse)


def head_kernel(
    info, pooled_in, gain_in, b_up_in, w_up, w_down, normed_out, own, partial, hidden_out,
    pooled, gain, b_up, up, down, normed, hidden, held, sems,
):
    loads = copied(
        sems, (pooled_in, pooled), (gain_in, gain), (b_up_in, b_up), (w_up, up), (w_down, down)
    )
    loads[0].wait()
    loads[1].wait()
    rows, width = pooled.shape
    quarter = own.shape[0]
    own[...] = pooled[pl.ds(pl.multiple_of(info[1] * quarter, quarter), quarter), :]
    values = pooled[...].astype(f32)
    center = values - jnp.mean(values, axis=-1, keepdims=True)
    spread = jnp.mean(center * center, axis=-1, keepdims=True)
    normed[...] = (center * lax.rsqrt(spread + 1e-06) * gain[...].reshape(1, width)).astype(bf16)
    store_normed = pltpu.make_async_copy(normed, normed_out, sems.at[5])
    store_normed.start()
    loads[2].wait()
    loads[3].wait()
    bias = b_up[...].reshape(1, b_up.shape[0])
    pre = jnp.dot(normed[...], up[...], preferred_element_type=f32) + bias
    hidden[...] = pre
    store_hidden = pltpu.make_async_copy(hidden, hidden_out, sems.at[6])
    store_hidden.start()
    tanh_value = jnp.tanh(root_two_pi * (pre + gelu_coeff * pre * pre * pre))
    activation = (0.5 * pre * (1.0 + tanh_value)).astype(bf16)
    loads[4].wait()
    held[...] = jnp.dot(activation, down[...], preferred_element_type=f32).astype(bf16)
    store = pltpu.make_async_copy(held, partial, sems.at[7])
    store.start()
    store_normed.wait()
    store_hidden.wait()
    store.wait()


def text_kernel(text, half):
    half[...] = unit_rows(text[...].astype(f32))[1].astype(bf16)


def select_kernel(info, normed, hidden, mine, theirs, slope_out, slope, sems):
    pre = hidden[...]
    square = pre * pre
    tanh_value = jnp.tanh(root_two_pi * (pre + gelu_coeff * square * pre))
    slope[...] = 0.5 * (1.0 + tanh_value) + 0.5 * pre * (1.0 - tanh_value * tanh_value) * (
        root_two_pi * (1.0 + 3.0 * gelu_coeff * square)
    )
    store = copied(sems, (slope, slope_out))[0]
    core = info[0]
    rows = 256
    count, width = mine.shape[0], normed.shape[1]
    normed_value = normed[...]
    for out, parity in ((mine, core), (theirs, 1 - core)):
        for start in range(0, count, rows):
            row = lax.broadcasted_iota(jnp.int32, (rows, 1), 0) + start
            chip = (row % (count // 2)) // 8
            within = jnp.where(row < count // 2, row % 8, 8)
            wanted = 18 * chip + 9 * parity + within
            feature = lax.broadcasted_iota(jnp.int32, (rows, width), 1)
            pick = jnp.where(feature == wanted, 1.0, 0.0).astype(bf16)
            out[start : start + rows, :] = dot(pick, normed_value, 1, 1).astype(bf16)
    store.wait()


def embed_kernel(parts, own, embedded_out, half_out, half, held, sems):
    embedded = own[...].astype(f32) + (
        (parts[0].astype(f32) + parts[1].astype(f32))
        + (parts[2].astype(f32) + parts[3].astype(f32))
    )
    half[...] = unit_rows(embedded)[1].astype(bf16)
    held[...] = embedded
    stores = copied(
        sems, *[(half, half_out.at[k]) for k in range(4)], (held, embedded_out)
    )
    for store in stores:
        store.wait()


def window_kernel(side_zero, pair, side_one, far, texts):
    count = pair.shape[0]
    texts[:count, :] = side_zero[...]
    texts[count : 2 * count, :] = pair[...]
    texts[2 * count : 3 * count, :] = side_one[...]
    texts[3 * count :, :] = far[...]


def positives(dims, image_dim, info, quarter):
    image = lax.broadcasted_iota(jnp.int32, dims, image_dim) - info[1] * quarter
    text = lax.broadcasted_iota(jnp.int32, dims, 1 - image_dim) - (2 + info[0]) * quarter
    return jnp.where((image == text) & (image >= 0) & (image < quarter), 1.0, 0.0)


def coefficients(logits, is_pair, scale):
    small = jnp.exp(-jnp.abs(logits))
    sigmoid = jnp.where(logits >= 0, 1.0, small) / (1.0 + small)
    return ((sigmoid - is_pair) * (scale / WINDOW)).astype(bf16), small


def image_kernel(info, factors, unit_half, texts, image_part, held, sems):
    scale, bias = factors[0], factors[1]
    quarter = texts.shape[0] // WINDOW
    window = texts[...]
    logits = scale * dot(unit_half[...], window, 1, 1) + bias
    is_pair = positives(logits.shape, 0, info, quarter)
    coefficient, _ = coefficients(logits, is_pair, scale)
    held[...] = dot(coefficient, window, 1, 0).astype(bf16)
    copied(sems, (held, image_part))[0].wait()


def text_part_kernel(info, factors, unit_half, texts, give, far_part, keep_side, keep_own):
    scale, bias = factors[0], factors[1]
    images = unit_half[...]
    q = texts.shape[0] // WINDOW
    width = images.shape[1]
    first = info[0] == 0
    logits = scale * dot(texts[...], images, 1, 1) + bias
    is_pair = positives(logits.shape, 1, info, q)
    coefficient, small = coefficients(logits, is_pair, scale)
    loss = jnp.maximum(logits, 0.0) + jnp.log1p(small) - is_pair * logits
    loss = jnp.sum(loss, axis=1, keepdims=True)
    lane = lax.broadcasted_iota(jnp.int32, (loss.shape[0], LANES), 1)
    for terms, cols in (
        (dot(coefficient, images, 1, 0), slice(0, width)),
        (jnp.where(lane == 0, loss, 0.0), slice(width, width + LANES)),
    ):
        left, right = terms[: 2 * q], terms[4 * q : 6 * q]
        one, two = terms[2 * q : 3 * q], terms[3 * q : 4 * q]
        keep_side[:, cols] = jnp.where(first, left, right)
        give[: 2 * q, cols] = jnp.where(first, right, left).astype(bf16)
        keep_own[:, cols] = jnp.where(first, one, two)
        give[2 * q :, cols] = jnp.where(first, two, one).astype(bf16)
        far_part[:, cols] = terms[6 * q :].astype(bf16)


def grad_kernel(parts, embedded_in, grad_out, embedded, grad, sems):
    load = copied(sems, (embedded_in, embedded))[0]
    grad_sum = (parts[0].astype(f32) + parts[1].astype(f32)) + (
        parts[2].astype(f32) + parts[3].astype(f32)
    )
    load.wait()
    inverse, unit_value = unit_rows(embedded[...])
    radial = jnp.sum(unit_value * grad_sum, axis=-1, keepdims=True)
    grad[...] = (inverse * (grad_sum - unit_value * radial)).astype(bf16)
    stores = copied(sems, *[(grad, grad_out.at[k]) for k in range(4)])
    for store in stores:
        store.wait()


def pre_kernel(grad_image, w_down, slope_in, grad_pre, slope, sems):
    load = copied(sems, (slope_in, slope))[0]
    grad_act = dot(grad_image[...], w_down[...], 1, 1)
    load.wait()
    grad_pre[...] = (grad_act * slope[...]).astype(bf16)


def up_kernel(info, mine, got, grads, wire):
    rows = grads.shape[0] // 2
    core = info[0]
    own = grads[pl.ds(pl.multiple_of(core * rows, rows), rows), :]
    other = grads[pl.ds(pl.multiple_of((1 - core) * rows, rows), rows), :]
    count = mine.shape[0] // 2
    chips = wire.shape[0]
    main = dot(mine[:count, :], own, 1, 0) + dot(got[:count, :], other, 1, 0)
    rest = dot(mine[count:, :], own, 1, 0) + dot(got[count:, :], other, 1, 0)
    place = lax.broadcasted_iota(jnp.int32, (count, LANES), 0) % 8
    blocks = [main[:, k * LANES : (k + 1) * LANES] for k in range(5)]
    ninth = jnp.zeros((count, LANES), f32)
    for k in range(5):
        ninth = jnp.where(place == k, rest[:, k * LANES : (k + 1) * LANES], ninth)
    blocks.append(ninth)
    for k in range(3):
        both = jnp.concatenate(
            [blocks[k].reshape(chips, 8, LANES), blocks[k + 3].reshape(chips, 8, LANES)], axis=1
        )
        wire[:, :, k * LANES : (k + 1) * LANES] = both.astype(bf16)


def up_sum_kernel(terms, up_grad):
    total = jnp.sum(terms[...].astype(f32), axis=0)
    up_grad[:8, : 3 * LANES] = total[:8, :]
    up_grad[:8, 3 * LANES :] = total[8:, : 2 * LANES]
    for k in range(5):
        up_grad[8:9, k * LANES : (k + 1) * LANES] = total[8 + k : 9 + k, 2 * LANES :]


def body(pooled, ln_gain, w_up, b_up, w_down, text, logit_scale, logit_bias):
    rows_count, width = pooled.shape
    q = text.shape[0]
    units = w_up.shape[1]
    core = lax.axis_index("c")
    first = core == 0
    info = jnp.stack([core, lax.axis_index("mp")]).astype(jnp.int32)
    factors = jnp.concatenate([logit_scale, logit_bias])
    wide = width + LANES

    def mp_exchange(partial):
        return lax.all_to_all(partial.reshape(4, q, width), "mp", 0, 0, tiled=True)

    whole = pltpu.HBM((rows_count, width), bf16)
    copies = pltpu.HBM((4, q, width), bf16)
    sems = pltpu.SemaphoreType.DMA((8,))

    normed, own, partial_out, hidden = call(
        head_kernel,
        (
            pltpu.HBM((rows_count, width), bf16),
            shape((q, width), bf16),
            pltpu.HBM((rows_count, width), bf16),
            pltpu.HBM((rows_count, units), f32),
        ),
        [SMEM] + [HBM] * 5,
        info,
        *(in_hbm(a) for a in (pooled, ln_gain, b_up, w_up, w_down)),
        specs=(HBM, VMEM, HBM, HBM),
        scratch=(
            pltpu.VMEM(pooled.shape, bf16),
            pltpu.VMEM((width,), f32),
            pltpu.VMEM((units,), f32),
            pltpu.VMEM(w_up.shape, bf16),
            pltpu.VMEM(w_down.shape, bf16),
            pltpu.VMEM(pooled.shape, bf16),
            pltpu.VMEM((rows_count, units), f32),
            pltpu.VMEM(pooled.shape, bf16),
            sems,
        ),
    )
    parts = mp_exchange(partial_out)

    text_half = call(text_kernel, shape((q, width), bf16), [VMEM], after(text, partial_out))
    pair = lax.all_gather(text_half, "c", axis=0, tiled=True)
    side_in = moved(pair, [(i, i + 2) if i % 2 == 0 else (i, i - 2) for i in range(N_DP)])
    far_out = [(i - 3, i) if i % 2 == 0 else (i + 3, i) for i in range(N_DP)]
    far = moved(text_half, far_out)

    embedded, image_half = call(
        embed_kernel,
        (pltpu.HBM((q, width), f32), copies),
        [VMEM, VMEM],
        parts,
        own,
        specs=(HBM, HBM),
        scratch=(pltpu.VMEM((q, width), bf16), pltpu.VMEM((q, width), f32), sems),
    )
    unit_half = mp_exchange(image_half).reshape(rows_count, width)

    sides = lax.all_gather(after(side_in, image_half), "c", axis=0, tiled=True)
    texts = call(
        window_kernel,
        shape((WINDOW * q, width), bf16),
        [VMEM] * 4,
        sides[: 2 * q],
        pair,
        sides[2 * q :],
        far,
    )

    half_rows = shape((1024, rows_count), bf16)
    mine, theirs, slope = call(
        select_kernel,
        (half_rows, half_rows, pltpu.HBM((rows_count, units), f32)),
        [SMEM, VMEM, VMEM],
        info,
        after(normed, image_half),
        hidden,
        specs=(VMEM, VMEM, HBM),
        scratch=(pltpu.VMEM((rows_count, units), f32), sems),
    )
    got_rows = swapped(theirs)
    texts = after(texts, theirs)

    image_part = call(
        image_kernel,
        whole,
        [SMEM, SMEM, VMEM, VMEM],
        info,
        factors,
        unit_half,
        texts,
        specs=HBM,
        scratch=(pltpu.VMEM((rows_count, width), bf16), sems),
    )
    grad_parts = mp_exchange(image_part)

    give, far_part, keep_side, keep_own = call(
        text_part_kernel,
        (
            shape((3 * q, wide), bf16),
            shape((q, wide), bf16),
            shape((2 * q, wide), f32),
            shape((q, wide), f32),
        ),
        [SMEM, SMEM, VMEM, VMEM],
        info,
        factors,
        after(unit_half, image_part),
        texts,
    )
    got = swapped(give).astype(f32)
    side = (keep_side + got[: 2 * q]).astype(bf16)
    own_sum = keep_own + got[2 * q :]

    grad_own = call(
        grad_kernel,
        copies,
        [VMEM, HBM],
        grad_parts,
        in_hbm(embedded),
        specs=HBM,
        scratch=(pltpu.VMEM((q, width), f32), pltpu.VMEM((q, width), bf16), sems),
    )
    grad_image = mp_exchange(grad_own).reshape(rows_count, width)
    side = after(side, grad_own)
    came = moved(side, [(i, i - 2) if i % 2 == 0 else (i, i + 2) for i in range(N_DP)])
    far_back = moved(after(far_part, grad_own), [(d, s) for s, d in far_out])

    grad_pre = call(
        pre_kernel,
        shape((rows_count, units), bf16),
        [VMEM, VMEM, HBM],
        grad_image,
        w_down,
        in_hbm(slope),
        scratch=(pltpu.VMEM((rows_count, units), f32), sems),
    )
    grads = lax.all_gather(grad_pre, "c", axis=0, tiled=True)
    up_wire = call(
        up_kernel,
        shape((N_DP // 2, 16, 3 * LANES), bf16),
        [SMEM] + [VMEM] * 3,
        info,
        mine,
        got_rows,
        grads,
    )
    up_terms = lax.all_to_all(up_wire, CHIPS, 0, 0, tiled=True)

    came = after(came, up_wire)
    came_first, came_second = came[:q], came[q:]
    last = swapped(jnp.where(first, came_second, came_first))
    total = (
        own_sum
        + jnp.where(first, came_first, came_second).astype(f32)
        + last.astype(f32)
        + far_back.astype(f32)
    )
    text_acc = total[:, :width]
    text_loss = total[:, width] / (WINDOW * rows_count)
    text_inv, text_unit = unit_rows(text.astype(f32))
    text_radial = jnp.sum(text_unit * text_acc, axis=-1, keepdims=True)
    text_grad = text_inv * (text_acc - text_unit * text_radial)

    up_grad = call(up_sum_kernel, shape((width // N_DP, units), f32), [VMEM], up_terms)
    return (up_grad, text_grad, text_loss)


def solution(mesh):
    fine = Mesh(mesh.devices.reshape(4, 2, 8, 2, 4), ("x", "zl", "y", "c", "mp"))
    every = (*DP, "mp")
    placed = (
        P(DP, None),
        P(),
        P(None, "mp"),
        P("mp"),
        P("mp", None),
        P(every, None),
        P(),
        P(),
    )
    return jax.shard_map(
        body,
        mesh=fine,
        in_specs=placed,
        out_specs=(P(DP, "mp"), P(every, None), P(every)),
        check_vma=False,
    )
```

```python
import math

import jax
import jax.numpy as jnp
from jax import lax
from jax.experimental import pallas as pl
from jax.experimental.pallas import tpu as pltpu
from jax.sharding import Mesh, PartitionSpec as P

REACH = 3
WINDOW = 2 * REACH + 1
CHIPS = ("x", "zl", "y")
DP = ("x", "zl", "y", "c")
N_DP = 128
LANES = 128

gelu_coeff = 0.044715
root_two_pi = math.sqrt(2.0 / math.pi)
f32 = jnp.float32
bf16 = jnp.bfloat16
VMEM = pl.BlockSpec(memory_space=pltpu.VMEM)
SMEM = pl.BlockSpec(memory_space=pltpu.SMEM)
HBM = pl.BlockSpec(memory_space=pltpu.HBM)


def shape(dims, kind):
    return jax.ShapeDtypeStruct(dims, kind)


def call(kernel, outs, ins, *args, scratch=(), specs=None):
    return pl.pallas_call(
        kernel,
        out_shape=outs,
        in_specs=ins,
        out_specs=specs if specs is not None else jax.tree.map(lambda _: VMEM, outs),
        scratch_shapes=list(scratch),
        cost_estimate=pl.CostEstimate(flops=1, transcendentals=0, bytes_accessed=1),
        compiler_params=pltpu.CompilerParams(vmem_limit_bytes=20 * 1024 * 1024),
    )(*args)


def copied(sems, *pairs):
    copies = [pltpu.make_async_copy(a, b, sems.at[k]) for k, (a, b) in enumerate(pairs)]
    for copy in copies:
        copy.start()
    return copies


def in_hbm(value):
    return pltpu.with_memory_space_constraint(value, pltpu.HBM)


def after(value, *earlier):
    return lax.optimization_barrier((value, *earlier))[0]


def moved(value, pairs):
    return lax.ppermute(value, DP, [(s % N_DP, d % N_DP) for s, d in pairs])


def swapped(value):
    return lax.ppermute(value, "c", [(0, 1), (1, 0)])


def of_both_cores(value):
    return lax.all_gather(value, "c", axis=0, tiled=True)


def dot(a, b, ca, cb):
    return lax.dot_general(a, b, (((ca,), (cb,)), ((), ())), preferred_element_type=f32)


def unit_rows(rows_float):
    inverse = lax.rsqrt(jnp.sum(rows_float * rows_float, axis=-1, keepdims=True) + 1e-06)
    return (inverse, rows_float * inverse)


def head_kernel(
    info, pooled_in, gain_in, b_up_in, w_up, w_down, normed_out, own, partial, hidden_out,
    pooled, gain, b_up, up, down, normed, hidden, held, sems,
):
    loads = copied(
        sems, (pooled_in, pooled), (gain_in, gain), (b_up_in, b_up), (w_up, up), (w_down, down)
    )
    loads[0].wait()
    loads[1].wait()
    rows, width = pooled.shape
    quarter = own.shape[0]
    own[...] = pooled[pl.ds(pl.multiple_of(info[1] * quarter, quarter), quarter), :]
    values = pooled[...].astype(f32)
    center = values - jnp.mean(values, axis=-1, keepdims=True)
    spread = jnp.mean(center * center, axis=-1, keepdims=True)
    normed[...] = (center * lax.rsqrt(spread + 1e-06) * gain[...].reshape(1, width)).astype(bf16)
    store_normed = pltpu.make_async_copy(normed, normed_out, sems.at[5])
    store_normed.start()
    loads[2].wait()
    loads[3].wait()
    bias = b_up[...].reshape(1, b_up.shape[0])
    pre = jnp.dot(normed[...], up[...], preferred_element_type=f32) + bias
    hidden[...] = pre
    store_hidden = pltpu.make_async_copy(hidden, hidden_out, sems.at[6])
    store_hidden.start()
    tanh_value = jnp.tanh(root_two_pi * (pre + gelu_coeff * pre * pre * pre))
    activation = (0.5 * pre * (1.0 + tanh_value)).astype(bf16)
    loads[4].wait()
    held[...] = jnp.dot(activation, down[...], preferred_element_type=f32).astype(bf16)
    store = pltpu.make_async_copy(held, partial, sems.at[7])
    store.start()
    store_normed.wait()
    store_hidden.wait()
    store.wait()


def text_kernel(text, half):
    half[...] = unit_rows(text[...].astype(f32))[1].astype(bf16)


def select_kernel(info, normed, hidden, mine, theirs, slope_out, slope, sems):
    pre = hidden[...]
    square = pre * pre
    tanh_value = jnp.tanh(root_two_pi * (pre + gelu_coeff * square * pre))
    slope[...] = 0.5 * (1.0 + tanh_value) + 0.5 * pre * (1.0 - tanh_value * tanh_value) * (
        root_two_pi * (1.0 + 3.0 * gelu_coeff * square)
    )
    store = copied(sems, (slope, slope_out))[0]
    core = info[0]
    rows = 256
    count, width = mine.shape[0], normed.shape[1]
    normed_value = normed[...]
    for out, parity in ((mine, core), (theirs, 1 - core)):
        for start in range(0, count, rows):
            row = lax.broadcasted_iota(jnp.int32, (rows, 1), 0) + start
            chip = (row % (count // 2)) // 8
            within = jnp.where(row < count // 2, row % 8, 8)
            wanted = 18 * chip + 9 * parity + within
            feature = lax.broadcasted_iota(jnp.int32, (rows, width), 1)
            pick = jnp.where(feature == wanted, 1.0, 0.0).astype(bf16)
            out[start : start + rows, :] = dot(pick, normed_value, 1, 1).astype(bf16)
    store.wait()


def embed_kernel(parts, own, embedded_out, half_out, half, held, sems):
    embedded = own[...].astype(f32) + (
        (parts[0].astype(f32) + parts[1].astype(f32))
        + (parts[2].astype(f32) + parts[3].astype(f32))
    )
    half[...] = unit_rows(embedded)[1].astype(bf16)
    held[...] = embedded
    stores = copied(
        sems, *[(half, half_out.at[k]) for k in range(4)], (held, embedded_out)
    )
    for store in stores:
        store.wait()


def window_kernel(side_zero, pair, side_one, far, texts):
    count = pair.shape[0]
    texts[:count, :] = side_zero[...]
    texts[count : 2 * count, :] = pair[...]
    texts[2 * count : 3 * count, :] = side_one[...]
    texts[3 * count :, :] = far[...]


def positives(dims, image_dim, info, quarter):
    image = lax.broadcasted_iota(jnp.int32, dims, image_dim) - info[1] * quarter
    text = lax.broadcasted_iota(jnp.int32, dims, 1 - image_dim) - (2 + info[0]) * quarter
    return jnp.where((image == text) & (image >= 0) & (image < quarter), 1.0, 0.0)


def coefficients(logits, is_pair, scale):
    small = jnp.exp(-jnp.abs(logits))
    sigmoid = jnp.where(logits >= 0, 1.0, small) / (1.0 + small)
    return ((sigmoid - is_pair) * (scale / WINDOW)).astype(bf16), small


def image_kernel(info, factors, unit_half, texts, image_part, held, sems):
    scale, bias = factors[0], factors[1]
    quarter = texts.shape[0] // WINDOW
    window = texts[...]
    logits = scale * dot(unit_half[...], window, 1, 1) + bias
    is_pair = positives(logits.shape, 0, info, quarter)
    coefficient, _ = coefficients(logits, is_pair, scale)
    held[...] = dot(coefficient, window, 1, 0).astype(bf16)
    copied(sems, (held, image_part))[0].wait()


def text_part_kernel(info, factors, unit_half, texts, give, far_part, keep_side, keep_own):
    scale, bias = factors[0], factors[1]
    images = unit_half[...]
    q = texts.shape[0] // WINDOW
    width = images.shape[1]
    first = info[0] == 0
    logits = scale * dot(texts[...], images, 1, 1) + bias
    is_pair = positives(logits.shape, 1, info, q)
    coefficient, small = coefficients(logits, is_pair, scale)
    loss = jnp.maximum(logits, 0.0) + jnp.log1p(small) - is_pair * logits
    loss = jnp.sum(loss, axis=1, keepdims=True)
    lane = lax.broadcasted_iota(jnp.int32, (loss.shape[0], LANES), 1)
    for terms, cols in (
        (dot(coefficient, images, 1, 0), slice(0, width)),
        (jnp.where(lane == 0, loss, 0.0), slice(width, width + LANES)),
    ):
        left, right = terms[: 2 * q], terms[4 * q : 6 * q]
        one, two = terms[2 * q : 3 * q], terms[3 * q : 4 * q]
        keep_side[:, cols] = jnp.where(first, left, right)
        give[: 2 * q, cols] = jnp.where(first, right, left).astype(bf16)
        keep_own[:, cols] = jnp.where(first, one, two)
        give[2 * q :, cols] = jnp.where(first, two, one).astype(bf16)
        far_part[:, cols] = terms[6 * q :].astype(bf16)


def side_kernel(info, gave, keep_side, keep_own, side, own_sum):
    q = keep_own.shape[0]
    start = pl.multiple_of((1 - info[0]) * 3 * q, 3 * q)
    side[...] = (keep_side[...] + gave[pl.ds(start, 2 * q), :].astype(f32)).astype(bf16)
    own_sum[...] = keep_own[...] + gave[pl.ds(start + 2 * q, q), :].astype(f32)


def text_grad_kernel(info, came, own_sum, far_back, text, text_grad, text_loss):
    q, width = text.shape
    start = pl.multiple_of(info[0] * q, q)
    total = (own_sum[...] + far_back[...].astype(f32)) + (
        came[pl.ds(start, q), :].astype(f32) + came[pl.ds(start + 2 * q, q), :].astype(f32)
    )
    inverse, unit_value = unit_rows(text[...].astype(f32))
    text_acc = total[:, :width]
    radial = jnp.sum(unit_value * text_acc, axis=-1, keepdims=True)
    text_grad[...] = inverse * (text_acc - unit_value * radial)
    text_loss[...] = total[:, width : width + 1] / (WINDOW * 4 * q)


def grad_kernel(parts, embedded_in, grad_out, embedded, grad, sems):
    load = copied(sems, (embedded_in, embedded))[0]
    grad_sum = (parts[0].astype(f32) + parts[1].astype(f32)) + (
        parts[2].astype(f32) + parts[3].astype(f32)
    )
    load.wait()
    inverse, unit_value = unit_rows(embedded[...])
    radial = jnp.sum(unit_value * grad_sum, axis=-1, keepdims=True)
    grad[...] = (inverse * (grad_sum - unit_value * radial)).astype(bf16)
    stores = copied(sems, *[(grad, grad_out.at[k]) for k in range(4)])
    for store in stores:
        store.wait()


def pre_kernel(grad_image, w_down, slope_in, grad_pre, slope, sems):
    load = copied(sems, (slope_in, slope))[0]
    grad_act = dot(grad_image[...], w_down[...], 1, 1)
    load.wait()
    grad_pre[...] = (grad_act * slope[...]).astype(bf16)


def up_kernel(info, mine, got, grads, wire):
    rows = grads.shape[0] // 2
    core = info[0]
    own = grads[pl.ds(pl.multiple_of(core * rows, rows), rows), :]
    other = grads[pl.ds(pl.multiple_of((1 - core) * rows, rows), rows), :]
    count = mine.shape[0] // 2
    chips = wire.shape[0]
    main = dot(mine[:count, :], own, 1, 0) + dot(got[:count, :], other, 1, 0)
    rest = dot(mine[count:, :], own, 1, 0) + dot(got[count:, :], other, 1, 0)
    place = lax.broadcasted_iota(jnp.int32, (count, LANES), 0) % 8
    blocks = [main[:, k * LANES : (k + 1) * LANES] for k in range(5)]
    ninth = jnp.zeros((count, LANES), f32)
    for k in range(5):
        ninth = jnp.where(place == k, rest[:, k * LANES : (k + 1) * LANES], ninth)
    blocks.append(ninth)
    for k in range(3):
        both = jnp.concatenate(
            [blocks[k].reshape(chips, 8, LANES), blocks[k + 3].reshape(chips, 8, LANES)], axis=1
        )
        wire[:, :, k * LANES : (k + 1) * LANES] = both.astype(bf16)


def up_sum_kernel(terms, up_grad):
    total = jnp.sum(terms[...].astype(f32), axis=0)
    up_grad[:8, : 3 * LANES] = total[:8, :]
    up_grad[:8, 3 * LANES :] = total[8:, : 2 * LANES]
    for k in range(5):
        up_grad[8:9, k * LANES : (k + 1) * LANES] = total[8 + k : 9 + k, 2 * LANES :]


def body(pooled, ln_gain, w_up, b_up, w_down, text, logit_scale, logit_bias):
    rows_count, width = pooled.shape
    q = text.shape[0]
    units = w_up.shape[1]
    core = lax.axis_index("c")
    info = jnp.stack([core, lax.axis_index("mp")]).astype(jnp.int32)
    factors = jnp.concatenate([logit_scale, logit_bias])
    wide = width + LANES

    def mp_exchange(partial):
        return lax.all_to_all(partial.reshape(4, q, width), "mp", 0, 0, tiled=True)

    whole = pltpu.HBM((rows_count, width), bf16)
    copies = pltpu.HBM((4, q, width), bf16)
    sems = pltpu.SemaphoreType.DMA((8,))

    normed, own, partial_out, hidden = call(
        head_kernel,
        (
            pltpu.HBM((rows_count, width), bf16),
            shape((q, width), bf16),
            pltpu.HBM((rows_count, width), bf16),
            pltpu.HBM((rows_count, units), f32),
        ),
        [SMEM] + [HBM] * 5,
        info,
        *(in_hbm(a) for a in (pooled, ln_gain, b_up, w_up, w_down)),
        specs=(HBM, VMEM, HBM, HBM),
        scratch=(
            pltpu.VMEM(pooled.shape, bf16),
            pltpu.VMEM((width,), f32),
            pltpu.VMEM((units,), f32),
            pltpu.VMEM(w_up.shape, bf16),
            pltpu.VMEM(w_down.shape, bf16),
            pltpu.VMEM(pooled.shape, bf16),
            pltpu.VMEM((rows_count, units), f32),
            pltpu.VMEM(pooled.shape, bf16),
            sems,
        ),
    )
    parts = mp_exchange(partial_out)

    text_half = call(text_kernel, shape((q, width), bf16), [VMEM], after(text, partial_out))
    pair = of_both_cores(text_half)
    side_in = moved(pair, [(i, i + 2) if i % 2 == 0 else (i, i - 2) for i in range(N_DP)])
    far_out = [(i - 3, i) if i % 2 == 0 else (i + 3, i) for i in range(N_DP)]
    far = moved(text_half, far_out)

    half_rows = shape((1024, rows_count), bf16)
    mine, theirs, slope = call(
        select_kernel,
        (half_rows, half_rows, pltpu.HBM((rows_count, units), f32)),
        [SMEM, VMEM, VMEM],
        info,
        normed,
        hidden,
        specs=(VMEM, VMEM, HBM),
        scratch=(pltpu.VMEM((rows_count, units), f32), sems),
    )

    embedded, image_half = call(
        embed_kernel,
        (pltpu.HBM((q, width), f32), copies),
        [VMEM, VMEM],
        parts,
        after(own, theirs, pair),
        specs=(HBM, HBM),
        scratch=(pltpu.VMEM((q, width), bf16), pltpu.VMEM((q, width), f32), sems),
    )
    unit_half = mp_exchange(image_half).reshape(rows_count, width)

    sides = of_both_cores(after(side_in, image_half))
    texts = call(
        window_kernel,
        shape((WINDOW * q, width), bf16),
        [VMEM] * 4,
        sides[: 2 * q],
        pair,
        sides[2 * q :],
        far,
    )

    got_rows = swapped(after(theirs, image_half))
    texts = after(texts, got_rows)

    image_part = call(
        image_kernel,
        whole,
        [SMEM, SMEM, VMEM, VMEM],
        info,
        factors,
        unit_half,
        texts,
        specs=HBM,
        scratch=(pltpu.VMEM((rows_count, width), bf16), sems),
    )
    grad_parts = mp_exchange(image_part)

    give, far_part, keep_side, keep_own = call(
        text_part_kernel,
        (
            shape((3 * q, wide), bf16),
            shape((q, wide), bf16),
            shape((2 * q, wide), f32),
            shape((q, wide), f32),
        ),
        [SMEM, SMEM, VMEM, VMEM],
        info,
        factors,
        after(unit_half, image_part),
        texts,
    )
    far_back = moved(after(far_part, grad_parts), [(d, s) for s, d in far_out])
    side, own_sum = call(
        side_kernel,
        (shape((2 * q, wide), bf16), shape((q, wide), f32)),
        [SMEM] + [VMEM] * 3,
        info,
        of_both_cores(give),
        keep_side,
        keep_own,
    )

    grad_own = call(
        grad_kernel,
        copies,
        [VMEM, HBM],
        after(grad_parts, side),
        in_hbm(embedded),
        specs=HBM,
        scratch=(pltpu.VMEM((q, width), f32), pltpu.VMEM((q, width), bf16), sems),
    )
    grad_image = mp_exchange(grad_own).reshape(rows_count, width)
    side = after(side, grad_own)
    came = moved(side, [(i, i - 2) if i % 2 == 0 else (i, i + 2) for i in range(N_DP)])

    grad_pre = call(
        pre_kernel,
        shape((rows_count, units), bf16),
        [VMEM, VMEM, HBM],
        grad_image,
        w_down,
        in_hbm(slope),
        scratch=(pltpu.VMEM((rows_count, units), f32), sems),
    )
    grads = of_both_cores(grad_pre)
    up_wire = call(
        up_kernel,
        shape((N_DP // 2, 16, 3 * LANES), bf16),
        [SMEM] + [VMEM] * 3,
        info,
        mine,
        got_rows,
        after(grads, came, far_back),
    )
    up_terms = lax.all_to_all(up_wire, CHIPS, 0, 0, tiled=True)

    text_grad, text_loss = call(
        text_grad_kernel,
        (shape((q, width), f32), shape((q, 1), f32)),
        [SMEM] + [VMEM] * 4,
        info,
        of_both_cores(after(came, up_wire)),
        own_sum,
        far_back,
        text,
    )
    text_loss = text_loss.reshape(q)

    up_grad = call(up_sum_kernel, shape((width // N_DP, units), f32), [VMEM], up_terms)
    return (up_grad, text_grad, text_loss)


def solution(mesh):
    fine = Mesh(mesh.devices.reshape(4, 2, 8, 2, 4), ("x", "zl", "y", "c", "mp"))
    every = (*DP, "mp")
    placed = (
        P(DP, None),
        P(),
        P(None, "mp"),
        P("mp"),
        P("mp", None),
        P(every, None),
        P(),
        P(),
    )
    return jax.shard_map(
        body,
        mesh=fine,
        in_specs=placed,
        out_specs=(P(DP, "mp"), P(every, None), P(every)),
        check_vma=False,
    )
```

```python
import math

import jax
import jax.numpy as jnp
from jax import lax
from jax.experimental import pallas as pl
from jax.experimental.pallas import tpu as pltpu
from jax.sharding import Mesh, PartitionSpec as P

REACH = 3
WINDOW = 2 * REACH + 1
CHIPS = ("x", "zl", "y")
DP = ("x", "zl", "y", "c")
N_DP = 128
LANES = 128

gelu_coeff = 0.044715
root_two_pi = math.sqrt(2.0 / math.pi)
f32 = jnp.float32
bf16 = jnp.bfloat16
VMEM = pl.BlockSpec(memory_space=pltpu.VMEM)
SMEM = pl.BlockSpec(memory_space=pltpu.SMEM)
HBM = pl.BlockSpec(memory_space=pltpu.HBM)


def shape(dims, kind):
    return jax.ShapeDtypeStruct(dims, kind)


def call(kernel, outs, ins, *args, scratch=(), specs=None):
    return pl.pallas_call(
        kernel,
        out_shape=outs,
        in_specs=ins,
        out_specs=specs if specs is not None else jax.tree.map(lambda _: VMEM, outs),
        scratch_shapes=list(scratch),
        cost_estimate=pl.CostEstimate(flops=1, transcendentals=0, bytes_accessed=1),
        compiler_params=pltpu.CompilerParams(vmem_limit_bytes=20 * 1024 * 1024),
    )(*args)


def copied(sems, *pairs):
    copies = [pltpu.make_async_copy(a, b, sems.at[k]) for k, (a, b) in enumerate(pairs)]
    for copy in copies:
        copy.start()
    return copies


def in_hbm(value):
    return pltpu.with_memory_space_constraint(value, pltpu.HBM)


def after(value, *earlier):
    return lax.optimization_barrier((value, *earlier))[0]


def moved(value, pairs):
    return lax.ppermute(value, DP, [(s % N_DP, d % N_DP) for s, d in pairs])


def swapped(value):
    return lax.ppermute(value, "c", [(0, 1), (1, 0)])


def of_both_cores(value):
    return lax.all_gather(value, "c", axis=0, tiled=True)


def dot(a, b, ca, cb):
    return lax.dot_general(a, b, (((ca,), (cb,)), ((), ())), preferred_element_type=f32)


def unit_rows(rows_float):
    inverse = lax.rsqrt(jnp.sum(rows_float * rows_float, axis=-1, keepdims=True) + 1e-06)
    return (inverse, rows_float * inverse)


def head_kernel(
    info, pooled_in, gain_in, b_up_in, w_up, w_down, normed_out, own, partial, hidden_out,
    pooled, gain, b_up, up, down, normed, hidden, held, sems,
):
    loads = copied(
        sems, (pooled_in, pooled), (gain_in, gain), (b_up_in, b_up), (w_up, up), (w_down, down)
    )
    loads[0].wait()
    loads[1].wait()
    rows, width = pooled.shape
    quarter = own.shape[0]
    own[...] = pooled[pl.ds(pl.multiple_of(info[1] * quarter, quarter), quarter), :]
    values = pooled[...].astype(f32)
    center = values - jnp.mean(values, axis=-1, keepdims=True)
    spread = jnp.mean(center * center, axis=-1, keepdims=True)
    normed[...] = (center * lax.rsqrt(spread + 1e-06) * gain[...].reshape(1, width)).astype(bf16)
    store_normed = pltpu.make_async_copy(normed, normed_out, sems.at[5])
    store_normed.start()
    loads[2].wait()
    loads[3].wait()
    bias = b_up[...].reshape(1, b_up.shape[0])
    pre = jnp.dot(normed[...], up[...], preferred_element_type=f32) + bias
    hidden[...] = pre
    store_hidden = pltpu.make_async_copy(hidden, hidden_out, sems.at[6])
    store_hidden.start()
    tanh_value = jnp.tanh(root_two_pi * (pre + gelu_coeff * pre * pre * pre))
    activation = (0.5 * pre * (1.0 + tanh_value)).astype(bf16)
    loads[4].wait()
    held[...] = jnp.dot(activation, down[...], preferred_element_type=f32).astype(bf16)
    store = pltpu.make_async_copy(held, partial, sems.at[7])
    store.start()
    store_normed.wait()
    store_hidden.wait()
    store.wait()


def text_kernel(text, half):
    half[...] = unit_rows(text[...].astype(f32))[1].astype(bf16)


def select_kernel(
    info, normed, hidden, mine_out, theirs_out, slope_out, mine, theirs, slope, sems
):
    pre = hidden[...]
    square = pre * pre
    tanh_value = jnp.tanh(root_two_pi * (pre + gelu_coeff * square * pre))
    slope[...] = 0.5 * (1.0 + tanh_value) + 0.5 * pre * (1.0 - tanh_value * tanh_value) * (
        root_two_pi * (1.0 + 3.0 * gelu_coeff * square)
    )
    stores = copied(sems, (slope, slope_out))
    core = info[0]
    rows = 256
    count, width = mine.shape[0], normed.shape[1]
    normed_value = normed[...]
    places = ((theirs, theirs_out, 1 - core), (mine, mine_out, core))
    for place, (out, target, parity) in enumerate(places):
        for start in range(0, count, rows):
            row = lax.broadcasted_iota(jnp.int32, (rows, 1), 0) + start
            chip = (row % (count // 2)) // 8
            within = jnp.where(row < count // 2, row % 8, 8)
            wanted = 18 * chip + 9 * parity + within
            feature = lax.broadcasted_iota(jnp.int32, (rows, width), 1)
            pick = jnp.where(feature == wanted, 1.0, 0.0).astype(bf16)
            out[start : start + rows, :] = dot(pick, normed_value, 1, 1).astype(bf16)
        stores.append(pltpu.make_async_copy(out, target, sems.at[1 + place]))
        stores[-1].start()
    for store in stores:
        store.wait()


def embed_kernel(parts, own, embedded_out, half_out, half, held, sems):
    embedded = own[...].astype(f32) + (
        (parts[0].astype(f32) + parts[1].astype(f32))
        + (parts[2].astype(f32) + parts[3].astype(f32))
    )
    half[...] = unit_rows(embedded)[1].astype(bf16)
    held[...] = embedded
    stores = copied(
        sems, *[(half, half_out.at[k]) for k in range(4)], (held, embedded_out)
    )
    for store in stores:
        store.wait()


def window_kernel(side_zero, pair, side_one, far, texts):
    count = pair.shape[0]
    texts[:count, :] = side_zero[...]
    texts[count : 2 * count, :] = pair[...]
    texts[2 * count : 3 * count, :] = side_one[...]
    texts[3 * count :, :] = far[...]


def positives(dims, image_dim, info, quarter):
    image = lax.broadcasted_iota(jnp.int32, dims, image_dim) - info[1] * quarter
    text = lax.broadcasted_iota(jnp.int32, dims, 1 - image_dim) - (2 + info[0]) * quarter
    return jnp.where((image == text) & (image >= 0) & (image < quarter), 1.0, 0.0)


def coefficients(logits, is_pair, scale):
    small = jnp.exp(-jnp.abs(logits))
    sigmoid = jnp.where(logits >= 0, 1.0, small) / (1.0 + small)
    return ((sigmoid - is_pair) * (scale / WINDOW)).astype(bf16), small


def image_kernel(info, factors, unit_half, texts, image_part, held, sems):
    scale, bias = factors[0], factors[1]
    quarter = texts.shape[0] // WINDOW
    window = texts[...]
    logits = scale * dot(unit_half[...], window, 1, 1) + bias
    is_pair = positives(logits.shape, 0, info, quarter)
    coefficient, _ = coefficients(logits, is_pair, scale)
    held[...] = dot(coefficient, window, 1, 0).astype(bf16)
    copied(sems, (held, image_part))[0].wait()


def text_part_kernel(info, factors, unit_half, texts, give, far_part, keep_side, keep_own):
    scale, bias = factors[0], factors[1]
    images = unit_half[...]
    q = texts.shape[0] // WINDOW
    width = images.shape[1]
    first = info[0] == 0
    logits = scale * dot(texts[...], images, 1, 1) + bias
    is_pair = positives(logits.shape, 1, info, q)
    coefficient, small = coefficients(logits, is_pair, scale)
    loss = jnp.maximum(logits, 0.0) + jnp.log1p(small) - is_pair * logits
    loss = jnp.sum(loss, axis=1, keepdims=True)
    lane = lax.broadcasted_iota(jnp.int32, (loss.shape[0], LANES), 1)
    for terms, cols in (
        (dot(coefficient, images, 1, 0), slice(0, width)),
        (jnp.where(lane == 0, loss, 0.0), slice(width, width + LANES)),
    ):
        left, right = terms[: 2 * q], terms[4 * q : 6 * q]
        one, two = terms[2 * q : 3 * q], terms[3 * q : 4 * q]
        keep_side[:, cols] = jnp.where(first, left, right)
        give[: 2 * q, cols] = jnp.where(first, right, left).astype(bf16)
        keep_own[:, cols] = jnp.where(first, one, two)
        give[2 * q :, cols] = jnp.where(first, two, one).astype(bf16)
        far_part[:, cols] = terms[6 * q :].astype(bf16)


def side_kernel(info, gave, far_got, keep_side, keep_own, side, own_sum):
    q = keep_own.shape[0]
    start = pl.multiple_of((1 - info[0]) * 3 * q, 3 * q)
    far = far_got[...].astype(f32)
    for half in range(2):
        rows = slice(half * q, (half + 1) * q)
        terms = keep_side[rows, :] + gave[pl.ds(start + half * q, q), :].astype(f32)
        side[rows, :] = (terms + jnp.where(info[0] == 1 - half, far, 0.0)).astype(bf16)
    own_sum[...] = keep_own[...] + gave[pl.ds(start + 2 * q, q), :].astype(f32)


def text_grad_kernel(info, came, own_sum, text, text_grad, text_loss):
    q, width = text.shape
    start = pl.multiple_of(info[0] * q, q)
    total = own_sum[...] + (
        came[pl.ds(start, q), :].astype(f32) + came[pl.ds(start + 2 * q, q), :].astype(f32)
    )
    inverse, unit_value = unit_rows(text[...].astype(f32))
    text_acc = total[:, :width]
    radial = jnp.sum(unit_value * text_acc, axis=-1, keepdims=True)
    text_grad[...] = inverse * (text_acc - unit_value * radial)
    text_loss[...] = total[:, width : width + 1] / (WINDOW * 4 * q)


def grad_kernel(parts, embedded_in, grad_out, embedded, grad, sems):
    load = copied(sems, (embedded_in, embedded))[0]
    grad_sum = (parts[0].astype(f32) + parts[1].astype(f32)) + (
        parts[2].astype(f32) + parts[3].astype(f32)
    )
    load.wait()
    inverse, unit_value = unit_rows(embedded[...])
    radial = jnp.sum(unit_value * grad_sum, axis=-1, keepdims=True)
    grad[...] = (inverse * (grad_sum - unit_value * radial)).astype(bf16)
    stores = copied(sems, *[(grad, grad_out.at[k]) for k in range(4)])
    for store in stores:
        store.wait()


def pre_kernel(grad_image, w_down, slope_in, grad_pre, slope, sems):
    load = copied(sems, (slope_in, slope))[0]
    grad_act = dot(grad_image[...], w_down[...], 1, 1)
    load.wait()
    grad_pre[...] = (grad_act * slope[...]).astype(bf16)


def up_kernel(info, mine, got, grads, wire):
    rows = grads.shape[0] // 2
    core = info[0]
    own = grads[pl.ds(pl.multiple_of(core * rows, rows), rows), :]
    other = grads[pl.ds(pl.multiple_of((1 - core) * rows, rows), rows), :]
    count = mine.shape[0] // 2
    chips = wire.shape[0]
    main = dot(mine[:count, :], own, 1, 0) + dot(got[:count, :], other, 1, 0)
    rest = dot(mine[count:, :], own, 1, 0) + dot(got[count:, :], other, 1, 0)
    place = lax.broadcasted_iota(jnp.int32, (count, LANES), 0) % 8
    blocks = [main[:, k * LANES : (k + 1) * LANES] for k in range(5)]
    ninth = jnp.zeros((count, LANES), f32)
    for k in range(5):
        ninth = jnp.where(place == k, rest[:, k * LANES : (k + 1) * LANES], ninth)
    blocks.append(ninth)
    for k in range(3):
        both = jnp.concatenate(
            [blocks[k].reshape(chips, 8, LANES), blocks[k + 3].reshape(chips, 8, LANES)], axis=1
        )
        wire[:, :, k * LANES : (k + 1) * LANES] = both.astype(bf16)


def up_sum_kernel(terms, up_grad):
    total = jnp.sum(terms[...].astype(f32), axis=0)
    up_grad[:8, : 3 * LANES] = total[:8, :]
    up_grad[:8, 3 * LANES :] = total[8:, : 2 * LANES]
    for k in range(5):
        up_grad[8:9, k * LANES : (k + 1) * LANES] = total[8 + k : 9 + k, 2 * LANES :]


def body(pooled, ln_gain, w_up, b_up, w_down, text, logit_scale, logit_bias):
    rows_count, width = pooled.shape
    q = text.shape[0]
    units = w_up.shape[1]
    core = lax.axis_index("c")
    info = jnp.stack([core, lax.axis_index("mp")]).astype(jnp.int32)
    factors = jnp.concatenate([logit_scale, logit_bias])
    wide = width + LANES

    def mp_exchange(partial):
        return lax.all_to_all(partial.reshape(4, q, width), "mp", 0, 0, tiled=True)

    whole = pltpu.HBM((rows_count, width), bf16)
    copies = pltpu.HBM((4, q, width), bf16)
    sems = pltpu.SemaphoreType.DMA((8,))

    normed, own, partial_out, hidden = call(
        head_kernel,
        (
            pltpu.HBM((rows_count, width), bf16),
            shape((q, width), bf16),
            pltpu.HBM((rows_count, width), bf16),
            pltpu.HBM((rows_count, units), f32),
        ),
        [SMEM] + [HBM] * 5,
        info,
        *(in_hbm(a) for a in (pooled, ln_gain, b_up, w_up, w_down)),
        specs=(HBM, VMEM, HBM, HBM),
        scratch=(
            pltpu.VMEM(pooled.shape, bf16),
            pltpu.VMEM((width,), f32),
            pltpu.VMEM((units,), f32),
            pltpu.VMEM(w_up.shape, bf16),
            pltpu.VMEM(w_down.shape, bf16),
            pltpu.VMEM(pooled.shape, bf16),
            pltpu.VMEM((rows_count, units), f32),
            pltpu.VMEM(pooled.shape, bf16),
            sems,
        ),
    )
    parts = mp_exchange(partial_out)

    text_half = call(text_kernel, shape((q, width), bf16), [VMEM], after(text, partial_out))
    pair = of_both_cores(text_half)
    inward = [(i, i + 2) if i % 2 == 0 else (i, i - 2) for i in range(N_DP)]
    outward = [(d, s) for s, d in inward]
    side_in = moved(pair, inward)

    half_rows = pltpu.HBM((1024, rows_count), bf16)
    mine, theirs, slope = call(
        select_kernel,
        (half_rows, half_rows, pltpu.HBM((rows_count, units), f32)),
        [SMEM, VMEM, VMEM],
        info,
        normed,
        hidden,
        specs=(HBM, HBM, HBM),
        scratch=(
            pltpu.VMEM((1024, rows_count), bf16),
            pltpu.VMEM((1024, rows_count), bf16),
            pltpu.VMEM((rows_count, units), f32),
            sems,
        ),
    )

    embedded, image_half = call(
        embed_kernel,
        (pltpu.HBM((q, width), f32), copies),
        [VMEM, VMEM],
        parts,
        after(own, theirs, pair),
        specs=(HBM, HBM),
        scratch=(pltpu.VMEM((q, width), bf16), pltpu.VMEM((q, width), f32), sems),
    )
    unit_half = mp_exchange(image_half).reshape(rows_count, width)

    side_in = after(side_in, image_half)
    far = moved(jnp.where(info[0] == 0, side_in[q:], side_in[:q]), inward)
    sides = of_both_cores(side_in)
    texts = call(
        window_kernel,
        shape((WINDOW * q, width), bf16),
        [VMEM] * 4,
        sides[: 2 * q],
        pair,
        sides[2 * q :],
        far,
    )

    got_rows = swapped(after(theirs, image_half))
    texts = after(texts, got_rows)

    image_part = call(
        image_kernel,
        whole,
        [SMEM, SMEM, VMEM, VMEM],
        info,
        factors,
        unit_half,
        texts,
        specs=HBM,
        scratch=(pltpu.VMEM((rows_count, width), bf16), sems),
    )
    grad_parts = mp_exchange(image_part)

    give, far_part, keep_side, keep_own = call(
        text_part_kernel,
        (
            shape((3 * q, wide), bf16),
            shape((q, wide), bf16),
            shape((2 * q, wide), f32),
            shape((q, wide), f32),
        ),
        [SMEM, SMEM, VMEM, VMEM],
        info,
        factors,
        after(unit_half, image_part),
        texts,
    )
    far_got = moved(far_part, outward)
    gave = of_both_cores(give)

    grad_own = call(
        grad_kernel,
        copies,
        [VMEM, HBM],
        after(grad_parts, gave, far_got),
        in_hbm(embedded),
        specs=HBM,
        scratch=(pltpu.VMEM((q, width), f32), pltpu.VMEM((q, width), bf16), sems),
    )
    grad_image = mp_exchange(grad_own).reshape(rows_count, width)
    side, own_sum = call(
        side_kernel,
        (shape((2 * q, wide), bf16), shape((q, wide), f32)),
        [SMEM] + [VMEM] * 4,
        info,
        after(gave, grad_own),
        far_got,
        keep_side,
        keep_own,
    )
    came = moved(side, outward)

    grad_pre = call(
        pre_kernel,
        shape((rows_count, units), bf16),
        [VMEM, VMEM, HBM],
        grad_image,
        w_down,
        in_hbm(slope),
        scratch=(pltpu.VMEM((rows_count, units), f32), sems),
    )
    grads = of_both_cores(grad_pre)
    up_wire = call(
        up_kernel,
        shape((N_DP // 2, 16, 3 * LANES), bf16),
        [SMEM] + [VMEM] * 3,
        info,
        mine,
        got_rows,
        after(grads, came),
    )
    up_terms = lax.all_to_all(up_wire, CHIPS, 0, 0, tiled=True)

    text_grad, text_loss = call(
        text_grad_kernel,
        (shape((q, width), f32), shape((q, 1), f32)),
        [SMEM] + [VMEM] * 3,
        info,
        of_both_cores(after(came, up_wire)),
        own_sum,
        text,
    )
    text_loss = text_loss.reshape(q)

    up_grad = call(up_sum_kernel, shape((width // N_DP, units), f32), [VMEM], up_terms)
    return (up_grad, text_grad, text_loss)


def solution(mesh):
    fine = Mesh(mesh.devices.reshape(4, 2, 8, 2, 4), ("x", "zl", "y", "c", "mp"))
    every = (*DP, "mp")
    placed = (
        P(DP, None),
        P(),
        P(None, "mp"),
        P("mp"),
        P("mp", None),
        P(every, None),
        P(),
        P(),
    )
    return jax.shard_map(
        body,
        mesh=fine,
        in_specs=placed,
        out_specs=(P(DP, "mp"), P(every, None), P(every)),
        check_vma=False,
    )
```

```python
import math

import jax
import jax.numpy as jnp
from jax import lax
from jax.experimental import pallas as pl
from jax.experimental.pallas import tpu as pltpu
from jax.sharding import Mesh, PartitionSpec as P

REACH = 3
WINDOW = 2 * REACH + 1
CHIPS = ("x", "zl", "y")
DP = ("x", "zl", "y", "c")
N_DP = 128
LANES = 128

gelu_coeff = 0.044715
root_two_pi = math.sqrt(2.0 / math.pi)
f32 = jnp.float32
bf16 = jnp.bfloat16
VMEM = pl.BlockSpec(memory_space=pltpu.VMEM)
SMEM = pl.BlockSpec(memory_space=pltpu.SMEM)
HBM = pl.BlockSpec(memory_space=pltpu.HBM)


def shape(dims, kind):
    return jax.ShapeDtypeStruct(dims, kind)


def call(kernel, outs, ins, *args, scratch=(), specs=None):
    return pl.pallas_call(
        kernel,
        out_shape=outs,
        in_specs=ins,
        out_specs=specs if specs is not None else jax.tree.map(lambda _: VMEM, outs),
        scratch_shapes=list(scratch),
        cost_estimate=pl.CostEstimate(flops=1, transcendentals=0, bytes_accessed=1),
        compiler_params=pltpu.CompilerParams(vmem_limit_bytes=20 * 1024 * 1024),
    )(*args)


def copied(sems, *pairs):
    copies = [pltpu.make_async_copy(a, b, sems.at[k]) for k, (a, b) in enumerate(pairs)]
    for copy in copies:
        copy.start()
    return copies


def in_hbm(value):
    return pltpu.with_memory_space_constraint(value, pltpu.HBM)


def after(value, *earlier):
    return lax.optimization_barrier((value, *earlier))[0]


def moved(value, pairs):
    return lax.ppermute(value, DP, [(s % N_DP, d % N_DP) for s, d in pairs])


def swapped(value):
    return lax.ppermute(value, "c", [(0, 1), (1, 0)])


def of_both_cores(value):
    return lax.all_gather(value, "c", axis=0, tiled=True)


def dot(a, b, ca, cb):
    return lax.dot_general(a, b, (((ca,), (cb,)), ((), ())), preferred_element_type=f32)


def unit_rows(rows_float):
    inverse = lax.rsqrt(jnp.sum(rows_float * rows_float, axis=-1, keepdims=True) + 1e-06)
    return (inverse, rows_float * inverse)


def head_kernel(
    info, pooled_in, gain_in, b_up_in, w_up, w_down, normed_out, own, partial, hidden_out,
    pooled, gain, b_up, up, down, normed, hidden, held, sems,
):
    loads = copied(
        sems, (pooled_in, pooled), (gain_in, gain), (b_up_in, b_up), (w_up, up), (w_down, down)
    )
    loads[0].wait()
    loads[1].wait()
    rows, width = pooled.shape
    quarter = own.shape[0]
    own[...] = pooled[pl.ds(pl.multiple_of(info[1] * quarter, quarter), quarter), :]
    values = pooled[...].astype(f32)
    center = values - jnp.mean(values, axis=-1, keepdims=True)
    spread = jnp.mean(center * center, axis=-1, keepdims=True)
    normed[...] = (center * lax.rsqrt(spread + 1e-06) * gain[...].reshape(1, width)).astype(bf16)
    store_normed = pltpu.make_async_copy(normed, normed_out, sems.at[5])
    store_normed.start()
    loads[2].wait()
    loads[3].wait()
    bias = b_up[...].reshape(1, b_up.shape[0])
    pre = jnp.dot(normed[...], up[...], preferred_element_type=f32) + bias
    hidden[...] = pre
    store_hidden = pltpu.make_async_copy(hidden, hidden_out, sems.at[6])
    store_hidden.start()
    tanh_value = jnp.tanh(root_two_pi * (pre + gelu_coeff * pre * pre * pre))
    activation = (0.5 * pre * (1.0 + tanh_value)).astype(bf16)
    loads[4].wait()
    held[...] = jnp.dot(activation, down[...], preferred_element_type=f32).astype(bf16)
    store = pltpu.make_async_copy(held, partial, sems.at[7])
    store.start()
    store_normed.wait()
    store_hidden.wait()
    store.wait()


def text_kernel(text, half):
    half[...] = unit_rows(text[...].astype(f32))[1].astype(bf16)


def select_kernel(info, normed, hidden, mine, theirs, slope_out, slope, sems):
    pre = hidden[...]
    square = pre * pre
    tanh_value = jnp.tanh(root_two_pi * (pre + gelu_coeff * square * pre))
    slope[...] = 0.5 * (1.0 + tanh_value) + 0.5 * pre * (1.0 - tanh_value * tanh_value) * (
        root_two_pi * (1.0 + 3.0 * gelu_coeff * square)
    )
    store = copied(sems, (slope, slope_out))[0]
    core = info[0]
    rows = 256
    count, width = mine.shape[0], normed.shape[1]
    normed_value = normed[...]
    for out, parity in ((mine, core), (theirs, 1 - core)):
        for start in range(0, count, rows):
            row = lax.broadcasted_iota(jnp.int32, (rows, 1), 0) + start
            chip = (row % (count // 2)) // 8
            within = jnp.where(row < count // 2, row % 8, 8)
            wanted = 18 * chip + 9 * parity + within
            feature = lax.broadcasted_iota(jnp.int32, (rows, width), 1)
            pick = jnp.where(feature == wanted, 1.0, 0.0).astype(bf16)
            out[start : start + rows, :] = dot(pick, normed_value, 1, 1).astype(bf16)
    store.wait()


def embed_kernel(parts, own, embedded_out, half_out, half, held, sems):
    embedded = own[...].astype(f32) + (
        (parts[0].astype(f32) + parts[1].astype(f32))
        + (parts[2].astype(f32) + parts[3].astype(f32))
    )
    half[...] = unit_rows(embedded)[1].astype(bf16)
    held[...] = embedded
    stores = copied(
        sems, *[(half, half_out.at[k]) for k in range(4)], (held, embedded_out)
    )
    for store in stores:
        store.wait()


def window_kernel(side_zero, pair, side_one, far, texts):
    count = pair.shape[0]
    texts[:count, :] = side_zero[...]
    texts[count : 2 * count, :] = pair[...]
    texts[2 * count : 3 * count, :] = side_one[...]
    texts[3 * count :, :] = far[...]


def positives(dims, image_dim, info, quarter):
    image = lax.broadcasted_iota(jnp.int32, dims, image_dim) - info[1] * quarter
    text = lax.broadcasted_iota(jnp.int32, dims, 1 - image_dim) - (2 + info[0]) * quarter
    return jnp.where((image == text) & (image >= 0) & (image < quarter), 1.0, 0.0)


def coefficients(logits, is_pair, scale):
    small = jnp.exp(-jnp.abs(logits))
    sigmoid = jnp.where(logits >= 0, 1.0, small) / (1.0 + small)
    return ((sigmoid - is_pair) * (scale / WINDOW)).astype(bf16), small


def image_kernel(info, factors, unit_half, texts, image_part, held, sems):
    scale, bias = factors[0], factors[1]
    quarter = texts.shape[0] // WINDOW
    window = texts[...]
    logits = scale * dot(unit_half[...], window, 1, 1) + bias
    is_pair = positives(logits.shape, 0, info, quarter)
    coefficient, _ = coefficients(logits, is_pair, scale)
    held[...] = dot(coefficient, window, 1, 0).astype(bf16)
    copied(sems, (held, image_part))[0].wait()


def text_part_kernel(info, factors, unit_half, texts, give, far_part, keep_side, keep_own):
    scale, bias = factors[0], factors[1]
    images = unit_half[...]
    q = texts.shape[0] // WINDOW
    width = images.shape[1]
    first = info[0] == 0
    logits = scale * dot(texts[...], images, 1, 1) + bias
    is_pair = positives(logits.shape, 1, info, q)
    coefficient, small = coefficients(logits, is_pair, scale)
    loss = jnp.maximum(logits, 0.0) + jnp.log1p(small) - is_pair * logits
    loss = jnp.sum(loss, axis=1, keepdims=True)
    lane = lax.broadcasted_iota(jnp.int32, (loss.shape[0], LANES), 1)
    for terms, cols in (
        (dot(coefficient, images, 1, 0), slice(0, width)),
        (jnp.where(lane == 0, loss, 0.0), slice(width, width + LANES)),
    ):
        left, right = terms[: 2 * q], terms[4 * q : 6 * q]
        one, two = terms[2 * q : 3 * q], terms[3 * q : 4 * q]
        keep_side[:, cols] = jnp.where(first, left, right)
        give[: 2 * q, cols] = jnp.where(first, right, left).astype(bf16)
        keep_own[:, cols] = jnp.where(first, one, two)
        give[2 * q :, cols] = jnp.where(first, two, one).astype(bf16)
        far_part[:, cols] = terms[6 * q :].astype(bf16)


def side_kernel(info, gave, keep_side, keep_own, side, own_sum):
    q = keep_own.shape[0]
    start = pl.multiple_of((1 - info[0]) * 3 * q, 3 * q)
    side[...] = (keep_side[...] + gave[pl.ds(start, 2 * q), :].astype(f32)).astype(bf16)
    own_sum[...] = keep_own[...] + gave[pl.ds(start + 2 * q, q), :].astype(f32)


def text_grad_kernel(info, came, own_sum, far_back, text, text_grad, text_loss):
    q, width = text.shape
    start = pl.multiple_of(info[0] * q, q)
    total = (own_sum[...] + far_back[...].astype(f32)) + (
        came[pl.ds(start, q), :].astype(f32) + came[pl.ds(start + 2 * q, q), :].astype(f32)
    )
    inverse, unit_value = unit_rows(text[...].astype(f32))
    text_acc = total[:, :width]
    radial = jnp.sum(unit_value * text_acc, axis=-1, keepdims=True)
    text_grad[...] = inverse * (text_acc - unit_value * radial)
    text_loss[...] = total[:, width : width + 1] / (WINDOW * 4 * q)


def grad_kernel(parts, embedded_in, grad_out, embedded, grad, sems):
    load = copied(sems, (embedded_in, embedded))[0]
    grad_sum = (parts[0].astype(f32) + parts[1].astype(f32)) + (
        parts[2].astype(f32) + parts[3].astype(f32)
    )
    load.wait()
    inverse, unit_value = unit_rows(embedded[...])
    radial = jnp.sum(unit_value * grad_sum, axis=-1, keepdims=True)
    grad[...] = (inverse * (grad_sum - unit_value * radial)).astype(bf16)
    stores = copied(sems, *[(grad, grad_out.at[k]) for k in range(4)])
    for store in stores:
        store.wait()


def pre_kernel(grad_image, w_down, slope_in, grad_pre, slope, sems):
    load = copied(sems, (slope_in, slope))[0]
    grad_act = dot(grad_image[...], w_down[...], 1, 1)
    load.wait()
    grad_pre[...] = (grad_act * slope[...]).astype(bf16)


def up_kernel(info, mine, got, grads, wire):
    rows = grads.shape[0] // 2
    core = info[0]
    own = grads[pl.ds(pl.multiple_of(core * rows, rows), rows), :]
    other = grads[pl.ds(pl.multiple_of((1 - core) * rows, rows), rows), :]
    count = mine.shape[0] // 2
    chips = wire.shape[0]
    main = dot(mine[:count, :], own, 1, 0) + dot(got[:count, :], other, 1, 0)
    rest = dot(mine[count:, :], own, 1, 0) + dot(got[count:, :], other, 1, 0)
    place = lax.broadcasted_iota(jnp.int32, (count, LANES), 0) % 8
    blocks = [main[:, k * LANES : (k + 1) * LANES] for k in range(5)]
    ninth = jnp.zeros((count, LANES), f32)
    for k in range(5):
        ninth = jnp.where(place == k, rest[:, k * LANES : (k + 1) * LANES], ninth)
    blocks.append(ninth)
    for k in range(3):
        both = jnp.concatenate(
            [blocks[k].reshape(chips, 8, LANES), blocks[k + 3].reshape(chips, 8, LANES)], axis=1
        )
        wire[:, :, k * LANES : (k + 1) * LANES] = both.astype(bf16)


def up_sum_kernel(terms, up_grad):
    total = jnp.sum(terms[...].astype(f32), axis=0)
    up_grad[:8, : 3 * LANES] = total[:8, :]
    up_grad[:8, 3 * LANES :] = total[8:, : 2 * LANES]
    for k in range(5):
        up_grad[8:9, k * LANES : (k + 1) * LANES] = total[8 + k : 9 + k, 2 * LANES :]


def body(pooled, ln_gain, w_up, b_up, w_down, text, logit_scale, logit_bias):
    rows_count, width = pooled.shape
    q = text.shape[0]
    units = w_up.shape[1]
    core = lax.axis_index("c")
    info = jnp.stack([core, lax.axis_index("mp")]).astype(jnp.int32)
    factors = jnp.concatenate([logit_scale, logit_bias])
    wide = width + LANES

    def mp_exchange(partial):
        return lax.all_to_all(partial.reshape(4, q, width), "mp", 0, 0, tiled=True)

    whole = pltpu.HBM((rows_count, width), bf16)
    copies = pltpu.HBM((4, q, width), bf16)
    sems = pltpu.SemaphoreType.DMA((8,))

    normed, own, partial_out, hidden = call(
        head_kernel,
        (
            pltpu.HBM((rows_count, width), bf16),
            shape((q, width), bf16),
            pltpu.HBM((rows_count, width), bf16),
            pltpu.HBM((rows_count, units), f32),
        ),
        [SMEM] + [HBM] * 5,
        info,
        *(in_hbm(a) for a in (pooled, ln_gain, b_up, w_up, w_down)),
        specs=(HBM, VMEM, HBM, HBM),
        scratch=(
            pltpu.VMEM(pooled.shape, bf16),
            pltpu.VMEM((width,), f32),
            pltpu.VMEM((units,), f32),
            pltpu.VMEM(w_up.shape, bf16),
            pltpu.VMEM(w_down.shape, bf16),
            pltpu.VMEM(pooled.shape, bf16),
            pltpu.VMEM((rows_count, units), f32),
            pltpu.VMEM(pooled.shape, bf16),
            sems,
        ),
    )
    parts = mp_exchange(partial_out)

    text_half = call(text_kernel, shape((q, width), bf16), [VMEM], after(text, partial_out))
    pair = of_both_cores(text_half)
    side_in = moved(pair, [(i, i + 2) if i % 2 == 0 else (i, i - 2) for i in range(N_DP)])
    far_out = [(i - 3, i) if i % 2 == 0 else (i + 3, i) for i in range(N_DP)]
    far = moved(text_half, far_out)

    half_rows = shape((1024, rows_count), bf16)
    mine, theirs, slope = call(
        select_kernel,
        (half_rows, half_rows, pltpu.HBM((rows_count, units), f32)),
        [SMEM, VMEM, VMEM],
        info,
        normed,
        hidden,
        specs=(VMEM, VMEM, HBM),
        scratch=(pltpu.VMEM((rows_count, units), f32), sems),
    )

    embedded, image_half = call(
        embed_kernel,
        (pltpu.HBM((q, width), f32), copies),
        [VMEM, VMEM],
        parts,
        after(own, theirs, pair),
        specs=(HBM, HBM),
        scratch=(pltpu.VMEM((q, width), bf16), pltpu.VMEM((q, width), f32), sems),
    )
    unit_half = mp_exchange(image_half).reshape(rows_count, width)

    sides = of_both_cores(after(side_in, image_half))
    texts = call(
        window_kernel,
        shape((WINDOW * q, width), bf16),
        [VMEM] * 4,
        sides[: 2 * q],
        pair,
        sides[2 * q :],
        far,
    )

    got_rows = swapped(after(theirs, image_half))
    texts = after(texts, got_rows)

    image_part = call(
        image_kernel,
        whole,
        [SMEM, SMEM, VMEM, VMEM],
        info,
        factors,
        unit_half,
        texts,
        specs=HBM,
        scratch=(pltpu.VMEM((rows_count, width), bf16), sems),
    )
    grad_parts = mp_exchange(image_part)

    give, far_part, keep_side, keep_own = call(
        text_part_kernel,
        (
            shape((3 * q, wide), bf16),
            shape((q, wide), bf16),
            shape((2 * q, wide), f32),
            shape((q, wide), f32),
        ),
        [SMEM, SMEM, VMEM, VMEM],
        info,
        factors,
        after(unit_half, image_part),
        texts,
    )
    far_back = moved(after(far_part, grad_parts), [(d, s) for s, d in far_out])
    side, own_sum = call(
        side_kernel,
        (shape((2 * q, wide), bf16), shape((q, wide), f32)),
        [SMEM] + [VMEM] * 3,
        info,
        of_both_cores(give),
        keep_side,
        keep_own,
    )

    grad_own = call(
        grad_kernel,
        copies,
        [VMEM, HBM],
        after(grad_parts, side),
        in_hbm(embedded),
        specs=HBM,
        scratch=(pltpu.VMEM((q, width), f32), pltpu.VMEM((q, width), bf16), sems),
    )
    grad_image = mp_exchange(grad_own).reshape(rows_count, width)
    side = after(side, grad_own)
    came = moved(side, [(i, i - 2) if i % 2 == 0 else (i, i + 2) for i in range(N_DP)])

    text_grad, text_loss = call(
        text_grad_kernel,
        (shape((q, width), f32), shape((q, 1), f32)),
        [SMEM] + [VMEM] * 4,
        info,
        of_both_cores(came),
        own_sum,
        far_back,
        text,
    )
    text_loss = text_loss.reshape(q)

    grad_image = after(grad_image, text_grad, text_loss)
    grad_pre = call(
        pre_kernel,
        shape((rows_count, units), bf16),
        [VMEM, VMEM, HBM],
        grad_image,
        w_down,
        in_hbm(slope),
        scratch=(pltpu.VMEM((rows_count, units), f32), sems),
    )
    grads = of_both_cores(grad_pre)
    up_wire = call(
        up_kernel,
        shape((N_DP // 2, 16, 3 * LANES), bf16),
        [SMEM] + [VMEM] * 3,
        info,
        mine,
        got_rows,
        grads,
    )
    up_terms = lax.all_to_all(up_wire, CHIPS, 0, 0, tiled=True)

    up_grad = call(up_sum_kernel, shape((width // N_DP, units), f32), [VMEM], up_terms)
    return (up_grad, text_grad, text_loss)


def solution(mesh):
    fine = Mesh(mesh.devices.reshape(4, 2, 8, 2, 4), ("x", "zl", "y", "c", "mp"))
    every = (*DP, "mp")
    placed = (
        P(DP, None),
        P(),
        P(None, "mp"),
        P("mp"),
        P("mp", None),
        P(every, None),
        P(),
        P(),
    )
    return jax.shard_map(
        body,
        mesh=fine,
        in_specs=placed,
        out_specs=(P(DP, "mp"), P(every, None), P(every)),
        check_vma=False,
    )
```

```python
import math

import jax
import jax.numpy as jnp
from jax import lax
from jax.experimental import pallas as pl
from jax.experimental.pallas import tpu as pltpu
from jax.sharding import Mesh, PartitionSpec as P

REACH = 3
WINDOW = 2 * REACH + 1
CHIPS = ("x", "zl", "y")
DP = ("x", "zl", "y", "c")
N_DP = 128
LANES = 128

gelu_coeff = 0.044715
root_two_pi = math.sqrt(2.0 / math.pi)
f32 = jnp.float32
bf16 = jnp.bfloat16
VMEM = pl.BlockSpec(memory_space=pltpu.VMEM)
SMEM = pl.BlockSpec(memory_space=pltpu.SMEM)
HBM = pl.BlockSpec(memory_space=pltpu.HBM)


def shape(dims, kind):
    return jax.ShapeDtypeStruct(dims, kind)


def call(kernel, outs, ins, *args, scratch=(), specs=None):
    return pl.pallas_call(
        kernel,
        out_shape=outs,
        in_specs=ins,
        out_specs=specs if specs is not None else jax.tree.map(lambda _: VMEM, outs),
        scratch_shapes=list(scratch),
        cost_estimate=pl.CostEstimate(flops=1, transcendentals=0, bytes_accessed=1),
        compiler_params=pltpu.CompilerParams(vmem_limit_bytes=20 * 1024 * 1024),
    )(*args)


def copied(sems, *pairs):
    copies = [pltpu.make_async_copy(a, b, sems.at[k]) for k, (a, b) in enumerate(pairs)]
    for copy in copies:
        copy.start()
    return copies


def in_hbm(value):
    return pltpu.with_memory_space_constraint(value, pltpu.HBM)


def after(value, *earlier):
    return lax.optimization_barrier((value, *earlier))[0]


def moved(value, pairs):
    return lax.ppermute(value, DP, [(s % N_DP, d % N_DP) for s, d in pairs])


def swapped(value):
    return lax.ppermute(value, "c", [(0, 1), (1, 0)])


def of_both_cores(value):
    return lax.all_gather(value, "c", axis=0, tiled=True)


def dot(a, b, ca, cb):
    return lax.dot_general(a, b, (((ca,), (cb,)), ((), ())), preferred_element_type=f32)


def unit_rows(rows_float):
    inverse = lax.rsqrt(jnp.sum(rows_float * rows_float, axis=-1, keepdims=True) + 1e-06)
    return (inverse, rows_float * inverse)


def head_kernel(
    info, pooled_in, gain_in, b_up_in, w_up, w_down, normed_out, own, partial, hidden_out,
    pooled, gain, b_up, up, down, normed, hidden, held, sems,
):
    loads = copied(
        sems, (pooled_in, pooled), (gain_in, gain), (b_up_in, b_up), (w_up, up), (w_down, down)
    )
    loads[0].wait()
    loads[1].wait()
    rows, width = pooled.shape
    quarter = own.shape[0]
    own[...] = pooled[pl.ds(pl.multiple_of(info[1] * quarter, quarter), quarter), :]
    values = pooled[...].astype(f32)
    center = values - jnp.mean(values, axis=-1, keepdims=True)
    spread = jnp.mean(center * center, axis=-1, keepdims=True)
    normed[...] = (center * lax.rsqrt(spread + 1e-06) * gain[...].reshape(1, width)).astype(bf16)
    store_normed = pltpu.make_async_copy(normed, normed_out, sems.at[5])
    store_normed.start()
    loads[2].wait()
    loads[3].wait()
    bias = b_up[...].reshape(1, b_up.shape[0])
    pre = jnp.dot(normed[...], up[...], preferred_element_type=f32) + bias
    hidden[...] = pre
    store_hidden = pltpu.make_async_copy(hidden, hidden_out, sems.at[6])
    store_hidden.start()
    tanh_value = jnp.tanh(root_two_pi * (pre + gelu_coeff * pre * pre * pre))
    activation = (0.5 * pre * (1.0 + tanh_value)).astype(bf16)
    loads[4].wait()
    held[...] = jnp.dot(activation, down[...], preferred_element_type=f32).astype(bf16)
    store = pltpu.make_async_copy(held, partial, sems.at[7])
    store.start()
    store_normed.wait()
    store_hidden.wait()
    store.wait()


def text_kernel(text, half):
    half[...] = unit_rows(text[...].astype(f32))[1].astype(bf16)


def select_kernel(info, normed, hidden, mine, theirs, slope_out, slope, sems):
    pre = hidden[...]
    square = pre * pre
    tanh_value = jnp.tanh(root_two_pi * (pre + gelu_coeff * square * pre))
    slope[...] = 0.5 * (1.0 + tanh_value) + 0.5 * pre * (1.0 - tanh_value * tanh_value) * (
        root_two_pi * (1.0 + 3.0 * gelu_coeff * square)
    )
    store = copied(sems, (slope, slope_out))[0]
    core = info[0]
    rows = 256
    count, width = mine.shape[0], normed.shape[1]
    normed_value = normed[...]
    for out, parity in ((mine, core), (theirs, 1 - core)):
        for start in range(0, count, rows):
            row = lax.broadcasted_iota(jnp.int32, (rows, 1), 0) + start
            chip = (row % (count // 2)) // 8
            within = jnp.where(row < count // 2, row % 8, 8)
            wanted = 18 * chip + 9 * parity + within
            feature = lax.broadcasted_iota(jnp.int32, (rows, width), 1)
            pick = jnp.where(feature == wanted, 1.0, 0.0).astype(bf16)
            out[start : start + rows, :] = dot(pick, normed_value, 1, 1).astype(bf16)
    store.wait()


def embed_kernel(parts, own, embedded_out, half_out, half, held, sems):
    embedded = own[...].astype(f32) + (
        (parts[0].astype(f32) + parts[1].astype(f32))
        + (parts[2].astype(f32) + parts[3].astype(f32))
    )
    half[...] = unit_rows(embedded)[1].astype(bf16)
    held[...] = embedded
    stores = copied(
        sems, *[(half, half_out.at[k]) for k in range(4)], (held, embedded_out)
    )
    for store in stores:
        store.wait()


def window_kernel(side_zero, pair, side_one, far, texts):
    count = pair.shape[0]
    texts[:count, :] = side_zero[...]
    texts[count : 2 * count, :] = pair[...]
    texts[2 * count : 3 * count, :] = side_one[...]
    texts[3 * count :, :] = far[...]


def positives(dims, image_dim, info, quarter):
    image = lax.broadcasted_iota(jnp.int32, dims, image_dim) - info[1] * quarter
    text = lax.broadcasted_iota(jnp.int32, dims, 1 - image_dim) - (2 + info[0]) * quarter
    return jnp.where((image == text) & (image >= 0) & (image < quarter), 1.0, 0.0)


def coefficients(logits, is_pair, scale):
    small = jnp.exp(-jnp.abs(logits))
    sigmoid = jnp.where(logits >= 0, 1.0, small) / (1.0 + small)
    return ((sigmoid - is_pair) * (scale / WINDOW)).astype(bf16), small


def image_kernel(info, logit_scale, logit_bias, unit_half, texts, image_part, held, sems):
    scale, bias = logit_scale[0], logit_bias[0]
    quarter = texts.shape[0] // WINDOW
    window = texts[...]
    logits = scale * dot(unit_half[...], window, 1, 1) + bias
    is_pair = positives(logits.shape, 0, info, quarter)
    coefficient, _ = coefficients(logits, is_pair, scale)
    held[...] = dot(coefficient, window, 1, 0).astype(bf16)
    copied(sems, (held, image_part))[0].wait()


def text_part_kernel(info, logit_scale, logit_bias, unit_half, texts, give, far_part, keep_side, keep_own):
    scale, bias = logit_scale[0], logit_bias[0]
    images = unit_half[...]
    q = texts.shape[0] // WINDOW
    width = images.shape[1]
    first = info[0] == 0
    logits = scale * dot(texts[...], images, 1, 1) + bias
    is_pair = positives(logits.shape, 1, info, q)
    coefficient, small = coefficients(logits, is_pair, scale)
    loss = jnp.maximum(logits, 0.0) + jnp.log1p(small) - is_pair * logits
    loss = jnp.sum(loss, axis=1, keepdims=True)
    lane = lax.broadcasted_iota(jnp.int32, (loss.shape[0], LANES), 1)
    for terms, cols in (
        (dot(coefficient, images, 1, 0), slice(0, width)),
        (jnp.where(lane == 0, loss, 0.0), slice(width, width + LANES)),
    ):
        left, right = terms[: 2 * q], terms[4 * q : 6 * q]
        one, two = terms[2 * q : 3 * q], terms[3 * q : 4 * q]
        keep_side[:, cols] = jnp.where(first, left, right)
        give[: 2 * q, cols] = jnp.where(first, right, left).astype(bf16)
        keep_own[:, cols] = jnp.where(first, one, two)
        give[2 * q :, cols] = jnp.where(first, two, one).astype(bf16)
        far_part[:, cols] = terms[6 * q :].astype(bf16)


def side_kernel(info, gave, keep_side, keep_own, side, own_sum):
    q = keep_own.shape[0]
    start = pl.multiple_of((1 - info[0]) * 3 * q, 3 * q)
    side[...] = (keep_side[...] + gave[pl.ds(start, 2 * q), :].astype(f32)).astype(bf16)
    own_sum[...] = keep_own[...] + gave[pl.ds(start + 2 * q, q), :].astype(f32)


def text_grad_kernel(info, came, own_sum, far_back, text, text_grad, text_loss):
    q, width = text.shape
    start = pl.multiple_of(info[0] * q, q)
    total = (own_sum[...] + far_back[...].astype(f32)) + (
        came[pl.ds(start, q), :].astype(f32) + came[pl.ds(start + 2 * q, q), :].astype(f32)
    )
    inverse, unit_value = unit_rows(text[...].astype(f32))
    text_acc = total[:, :width]
    radial = jnp.sum(unit_value * text_acc, axis=-1, keepdims=True)
    text_grad[...] = inverse * (text_acc - unit_value * radial)
    text_loss[...] = total[:, width : width + 1] / (WINDOW * 4 * q)


def grad_kernel(parts, embedded_in, grad_out, embedded, grad, sems):
    load = copied(sems, (embedded_in, embedded))[0]
    grad_sum = (parts[0].astype(f32) + parts[1].astype(f32)) + (
        parts[2].astype(f32) + parts[3].astype(f32)
    )
    load.wait()
    inverse, unit_value = unit_rows(embedded[...])
    radial = jnp.sum(unit_value * grad_sum, axis=-1, keepdims=True)
    grad[...] = (inverse * (grad_sum - unit_value * radial)).astype(bf16)
    stores = copied(sems, *[(grad, grad_out.at[k]) for k in range(4)])
    for store in stores:
        store.wait()


def pre_kernel(grad_image, w_down, slope_in, grad_pre, slope, sems):
    load = copied(sems, (slope_in, slope))[0]
    grad_act = dot(grad_image[...], w_down[...], 1, 1)
    load.wait()
    grad_pre[...] = (grad_act * slope[...]).astype(bf16)


def up_kernel(info, mine, got, grads, wire):
    rows = grads.shape[0] // 2
    core = info[0]
    own = grads[pl.ds(pl.multiple_of(core * rows, rows), rows), :]
    other = grads[pl.ds(pl.multiple_of((1 - core) * rows, rows), rows), :]
    count = mine.shape[0] // 2
    chips = wire.shape[0]
    main = dot(mine[:count, :], own, 1, 0) + dot(got[:count, :], other, 1, 0)
    rest = dot(mine[count:, :], own, 1, 0) + dot(got[count:, :], other, 1, 0)
    place = lax.broadcasted_iota(jnp.int32, (count, LANES), 0) % 8
    blocks = [main[:, k * LANES : (k + 1) * LANES] for k in range(5)]
    ninth = jnp.zeros((count, LANES), f32)
    for k in range(5):
        ninth = jnp.where(place == k, rest[:, k * LANES : (k + 1) * LANES], ninth)
    blocks.append(ninth)
    for k in range(3):
        both = jnp.concatenate(
            [blocks[k].reshape(chips, 8, LANES), blocks[k + 3].reshape(chips, 8, LANES)], axis=1
        )
        wire[:, :, k * LANES : (k + 1) * LANES] = both.astype(bf16)


def up_sum_kernel(terms, up_grad):
    total = jnp.sum(terms[...].astype(f32), axis=0)
    up_grad[:8, : 3 * LANES] = total[:8, :]
    up_grad[:8, 3 * LANES :] = total[8:, : 2 * LANES]
    for k in range(5):
        up_grad[8:9, k * LANES : (k + 1) * LANES] = total[8 + k : 9 + k, 2 * LANES :]


def body(pooled, ln_gain, w_up, b_up, w_down, text, logit_scale, logit_bias):
    rows_count, width = pooled.shape
    q = text.shape[0]
    units = w_up.shape[1]
    core = lax.axis_index("c")
    info = jnp.stack([core, lax.axis_index("mp")]).astype(jnp.int32)
    wide = width + LANES

    def mp_exchange(partial):
        return lax.all_to_all(partial.reshape(4, q, width), "mp", 0, 0, tiled=True)

    whole = pltpu.HBM((rows_count, width), bf16)
    copies = pltpu.HBM((4, q, width), bf16)
    sems = pltpu.SemaphoreType.DMA((8,))

    normed, own, partial_out, hidden = call(
        head_kernel,
        (
            pltpu.HBM((rows_count, width), bf16),
            shape((q, width), bf16),
            pltpu.HBM((rows_count, width), bf16),
            pltpu.HBM((rows_count, units), f32),
        ),
        [SMEM] + [HBM] * 5,
        info,
        *(in_hbm(a) for a in (pooled, ln_gain, b_up, w_up, w_down)),
        specs=(HBM, VMEM, HBM, HBM),
        scratch=(
            pltpu.VMEM(pooled.shape, bf16),
            pltpu.VMEM((width,), f32),
            pltpu.VMEM((units,), f32),
            pltpu.VMEM(w_up.shape, bf16),
            pltpu.VMEM(w_down.shape, bf16),
            pltpu.VMEM(pooled.shape, bf16),
            pltpu.VMEM((rows_count, units), f32),
            pltpu.VMEM(pooled.shape, bf16),
            sems,
        ),
    )
    parts = mp_exchange(partial_out)

    text_half = call(text_kernel, shape((q, width), bf16), [VMEM], after(text, partial_out))
    pair = of_both_cores(text_half)
    side_in = moved(pair, [(i, i + 2) if i % 2 == 0 else (i, i - 2) for i in range(N_DP)])
    far_out = [(i - 3, i) if i % 2 == 0 else (i + 3, i) for i in range(N_DP)]
    far = moved(text_half, far_out)

    half_rows = shape((1024, rows_count), bf16)
    mine, theirs, slope = call(
        select_kernel,
        (half_rows, half_rows, pltpu.HBM((rows_count, units), f32)),
        [SMEM, VMEM, VMEM],
        info,
        normed,
        hidden,
        specs=(VMEM, VMEM, HBM),
        scratch=(pltpu.VMEM((rows_count, units), f32), sems),
    )

    embedded, image_half = call(
        embed_kernel,
        (pltpu.HBM((q, width), f32), copies),
        [VMEM, VMEM],
        parts,
        after(own, theirs, pair, far),
        specs=(HBM, HBM),
        scratch=(pltpu.VMEM((q, width), bf16), pltpu.VMEM((q, width), f32), sems),
    )
    unit_half = mp_exchange(image_half).reshape(rows_count, width)

    sides = of_both_cores(after(side_in, image_half))
    texts = call(
        window_kernel,
        shape((WINDOW * q, width), bf16),
        [VMEM] * 4,
        sides[: 2 * q],
        pair,
        sides[2 * q :],
        far,
    )


    image_part = call(
        image_kernel,
        whole,
        [SMEM] * 3 + [VMEM] * 2,
        info,
        logit_scale,
        logit_bias,
        unit_half,
        texts,
        specs=HBM,
        scratch=(pltpu.VMEM((rows_count, width), bf16), sems),
    )
    grad_parts = mp_exchange(image_part)
    got_rows = swapped(after(theirs, image_part))

    give, far_part, keep_side, keep_own = call(
        text_part_kernel,
        (
            shape((3 * q, wide), bf16),
            shape((q, wide), bf16),
            shape((2 * q, wide), f32),
            shape((q, wide), f32),
        ),
        [SMEM] * 3 + [VMEM] * 2,
        info,
        logit_scale,
        logit_bias,
        after(unit_half, image_part),
        texts,
    )
    far_back = moved(after(far_part, grad_parts), [(d, s) for s, d in far_out])
    side, own_sum = call(
        side_kernel,
        (shape((2 * q, wide), bf16), shape((q, wide), f32)),
        [SMEM] + [VMEM] * 3,
        info,
        of_both_cores(give),
        keep_side,
        keep_own,
    )

    grad_own = call(
        grad_kernel,
        copies,
        [VMEM, HBM],
        after(grad_parts, side),
        in_hbm(embedded),
        specs=HBM,
        scratch=(pltpu.VMEM((q, width), f32), pltpu.VMEM((q, width), bf16), sems),
    )
    grad_image = mp_exchange(grad_own).reshape(rows_count, width)
    side = after(side, grad_own)
    came = moved(side, [(i, i - 2) if i % 2 == 0 else (i, i + 2) for i in range(N_DP)])

    grad_pre = call(
        pre_kernel,
        shape((rows_count, units), bf16),
        [VMEM, VMEM, HBM],
        grad_image,
        w_down,
        in_hbm(slope),
        scratch=(pltpu.VMEM((rows_count, units), f32), sems),
    )
    grads = of_both_cores(grad_pre)
    up_wire = call(
        up_kernel,
        shape((N_DP // 2, 16, 3 * LANES), bf16),
        [SMEM] + [VMEM] * 3,
        info,
        mine,
        got_rows,
        after(grads, came, far_back),
    )
    up_terms = lax.all_to_all(up_wire, CHIPS, 0, 0, tiled=True)

    text_grad, text_loss = call(
        text_grad_kernel,
        (shape((q, width), f32), shape((q, 1), f32)),
        [SMEM] + [VMEM] * 4,
        info,
        of_both_cores(after(came, up_wire)),
        own_sum,
        far_back,
        text,
    )
    text_loss = text_loss.reshape(q)

    up_grad = call(up_sum_kernel, shape((width // N_DP, units), f32), [VMEM], up_terms)
    return (up_grad, text_grad, text_loss)


def solution(mesh):
    fine = Mesh(mesh.devices.reshape(4, 2, 8, 2, 4), ("x", "zl", "y", "c", "mp"))
    every = (*DP, "mp")
    placed = (
        P(DP, None),
        P(),
        P(None, "mp"),
        P("mp"),
        P("mp", None),
        P(every, None),
        P(),
        P(),
    )
    return jax.shard_map(
        body,
        mesh=fine,
        in_specs=placed,
        out_specs=(P(DP, "mp"), P(every, None), P(every)),
        check_vma=False,
    )
```

```python
import math

import jax
import jax.numpy as jnp
from jax import lax
from jax.experimental import pallas as pl
from jax.experimental.pallas import tpu as pltpu
from jax.sharding import Mesh, PartitionSpec as P

REACH = 3
WINDOW = 2 * REACH + 1
CHIPS = ("x", "zl", "y")
DP = ("x", "zl", "y", "c")
N_DP = 128
LANES = 128

gelu_coeff = 0.044715
root_two_pi = math.sqrt(2.0 / math.pi)
f32 = jnp.float32
bf16 = jnp.bfloat16
VMEM = pl.BlockSpec(memory_space=pltpu.VMEM)
SMEM = pl.BlockSpec(memory_space=pltpu.SMEM)
HBM = pl.BlockSpec(memory_space=pltpu.HBM)


def shape(dims, kind):
    return jax.ShapeDtypeStruct(dims, kind)


def call(kernel, outs, ins, *args, scratch=(), specs=None):
    return pl.pallas_call(
        kernel,
        out_shape=outs,
        in_specs=ins,
        out_specs=specs if specs is not None else jax.tree.map(lambda _: VMEM, outs),
        scratch_shapes=list(scratch),
        cost_estimate=pl.CostEstimate(flops=1, transcendentals=0, bytes_accessed=1),
        compiler_params=pltpu.CompilerParams(vmem_limit_bytes=20 * 1024 * 1024),
    )(*args)


def copied(sems, *pairs):
    copies = [pltpu.make_async_copy(a, b, sems.at[k]) for k, (a, b) in enumerate(pairs)]
    for copy in copies:
        copy.start()
    return copies


def in_hbm(value):
    return pltpu.with_memory_space_constraint(value, pltpu.HBM)


def after(value, *earlier):
    return lax.optimization_barrier((value, *earlier))[0]


def moved(value, pairs):
    return lax.ppermute(value, DP, [(s % N_DP, d % N_DP) for s, d in pairs])


def swapped(value):
    return lax.ppermute(value, "c", [(0, 1), (1, 0)])


def of_both_cores(value):
    return lax.all_gather(value, "c", axis=0, tiled=True)


def dot(a, b, ca, cb):
    return lax.dot_general(a, b, (((ca,), (cb,)), ((), ())), preferred_element_type=f32)


def unit_rows(rows_float):
    inverse = lax.rsqrt(jnp.sum(rows_float * rows_float, axis=-1, keepdims=True) + 1e-06)
    return (inverse, rows_float * inverse)


def head_kernel(
    info, pooled_in, gain_in, b_up_in, w_up, w_down, normed_out, own, partial, hidden_out,
    pooled, gain, b_up, up, down, normed, hidden, held, sems,
):
    loads = copied(
        sems, (pooled_in, pooled), (gain_in, gain), (b_up_in, b_up), (w_up, up), (w_down, down)
    )
    loads[0].wait()
    loads[1].wait()
    rows, width = pooled.shape
    quarter = own.shape[0]
    own[...] = pooled[pl.ds(pl.multiple_of(info[1] * quarter, quarter), quarter), :]
    values = pooled[...].astype(f32)
    center = values - jnp.mean(values, axis=-1, keepdims=True)
    spread = jnp.mean(center * center, axis=-1, keepdims=True)
    normed[...] = (center * lax.rsqrt(spread + 1e-06) * gain[...].reshape(1, width)).astype(bf16)
    store_normed = pltpu.make_async_copy(normed, normed_out, sems.at[5])
    store_normed.start()
    loads[2].wait()
    loads[3].wait()
    bias = b_up[...].reshape(1, b_up.shape[0])
    pre = jnp.dot(normed[...], up[...], preferred_element_type=f32) + bias
    hidden[...] = pre
    store_hidden = pltpu.make_async_copy(hidden, hidden_out, sems.at[6])
    store_hidden.start()
    tanh_value = jnp.tanh(root_two_pi * (pre + gelu_coeff * pre * pre * pre))
    activation = (0.5 * pre * (1.0 + tanh_value)).astype(bf16)
    loads[4].wait()
    held[...] = jnp.dot(activation, down[...], preferred_element_type=f32).astype(bf16)
    store = pltpu.make_async_copy(held, partial, sems.at[7])
    store.start()
    store_normed.wait()
    store_hidden.wait()
    store.wait()


def text_kernel(text, half):
    half[...] = unit_rows(text[...].astype(f32))[1].astype(bf16)


def select_kernel(info, normed, hidden, mine, theirs, slope_out, slope, sems):
    pre = hidden[...]
    square = pre * pre
    tanh_value = jnp.tanh(root_two_pi * (pre + gelu_coeff * square * pre))
    slope[...] = 0.5 * (1.0 + tanh_value) + 0.5 * pre * (1.0 - tanh_value * tanh_value) * (
        root_two_pi * (1.0 + 3.0 * gelu_coeff * square)
    )
    store = copied(sems, (slope, slope_out))[0]
    core = info[0]
    rows = 256
    count, width = mine.shape[0], normed.shape[1]
    normed_value = normed[...]
    for out, parity in ((mine, core), (theirs, 1 - core)):
        for start in range(0, count, rows):
            row = lax.broadcasted_iota(jnp.int32, (rows, 1), 0) + start
            chip = (row % (count // 2)) // 8
            within = jnp.where(row < count // 2, row % 8, 8)
            wanted = 18 * chip + 9 * parity + within
            feature = lax.broadcasted_iota(jnp.int32, (rows, width), 1)
            pick = jnp.where(feature == wanted, 1.0, 0.0).astype(bf16)
            out[start : start + rows, :] = dot(pick, normed_value, 1, 1).astype(bf16)
    store.wait()


def embed_kernel(parts, own, embedded_out, half_out, half, held, sems):
    embedded = own[...].astype(f32) + (
        (parts[0].astype(f32) + parts[1].astype(f32))
        + (parts[2].astype(f32) + parts[3].astype(f32))
    )
    half[...] = unit_rows(embedded)[1].astype(bf16)
    held[...] = embedded
    stores = copied(
        sems, *[(half, half_out.at[k]) for k in range(4)], (held, embedded_out)
    )
    for store in stores:
        store.wait()


def window_kernel(side_zero, pair, side_one, far, texts):
    count = pair.shape[0]
    texts[:count, :] = side_zero[...]
    texts[count : 2 * count, :] = pair[...]
    texts[2 * count : 3 * count, :] = side_one[...]
    texts[3 * count :, :] = far[...]


def positives(dims, image_dim, info, quarter):
    image = lax.broadcasted_iota(jnp.int32, dims, image_dim) - info[1] * quarter
    text = lax.broadcasted_iota(jnp.int32, dims, 1 - image_dim) - (2 + info[0]) * quarter
    return jnp.where((image == text) & (image >= 0) & (image < quarter), 1.0, 0.0)


def coefficients(logits, is_pair, scale):
    small = jnp.exp(-jnp.abs(logits))
    sigmoid = jnp.where(logits >= 0, 1.0, small) / (1.0 + small)
    return ((sigmoid - is_pair) * (scale / WINDOW)).astype(bf16), small


def image_kernel(info, logit_scale, logit_bias, unit_half, texts, image_part, held, sems):
    scale, bias = logit_scale[0], logit_bias[0]
    quarter = texts.shape[0] // WINDOW
    window = texts[...]
    logits = scale * dot(unit_half[...], window, 1, 1) + bias
    is_pair = positives(logits.shape, 0, info, quarter)
    coefficient, _ = coefficients(logits, is_pair, scale)
    held[...] = dot(coefficient, window, 1, 0).astype(bf16)
    copied(sems, (held, image_part))[0].wait()


def text_part_kernel(info, logit_scale, logit_bias, unit_half, texts, give, far_part, keep_side, keep_own):
    scale, bias = logit_scale[0], logit_bias[0]
    images = unit_half[...]
    q = texts.shape[0] // WINDOW
    width = images.shape[1]
    first = info[0] == 0
    logits = scale * dot(texts[...], images, 1, 1) + bias
    is_pair = positives(logits.shape, 1, info, q)
    coefficient, small = coefficients(logits, is_pair, scale)
    loss = jnp.maximum(logits, 0.0) + jnp.log1p(small) - is_pair * logits
    loss = jnp.sum(loss, axis=1, keepdims=True)
    lane = lax.broadcasted_iota(jnp.int32, (loss.shape[0], LANES), 1)
    for terms, cols in (
        (dot(coefficient, images, 1, 0), slice(0, width)),
        (jnp.where(lane == 0, loss, 0.0), slice(width, width + LANES)),
    ):
        left, right = terms[: 2 * q], terms[4 * q : 6 * q]
        one, two = terms[2 * q : 3 * q], terms[3 * q : 4 * q]
        keep_side[:, cols] = jnp.where(first, left, right)
        give[: 2 * q, cols] = jnp.where(first, right, left).astype(bf16)
        keep_own[:, cols] = jnp.where(first, one, two)
        give[2 * q :, cols] = jnp.where(first, two, one).astype(bf16)
        far_part[:, cols] = terms[6 * q :].astype(bf16)


def side_kernel(info, gave, keep_side, keep_own, side, own_sum):
    q = keep_own.shape[0]
    start = pl.multiple_of((1 - info[0]) * 3 * q, 3 * q)
    side[...] = (keep_side[...] + gave[pl.ds(start, 2 * q), :].astype(f32)).astype(bf16)
    own_sum[...] = keep_own[...] + gave[pl.ds(start + 2 * q, q), :].astype(f32)


def text_grad_kernel(info, came, own_sum, far_back, text, text_grad, text_loss):
    q, width = text.shape
    start = pl.multiple_of(info[0] * q, q)
    total = (own_sum[...] + far_back[...].astype(f32)) + (
        came[pl.ds(start, q), :].astype(f32) + came[pl.ds(start + 2 * q, q), :].astype(f32)
    )
    inverse, unit_value = unit_rows(text[...].astype(f32))
    text_acc = total[:, :width]
    radial = jnp.sum(unit_value * text_acc, axis=-1, keepdims=True)
    text_grad[...] = inverse * (text_acc - unit_value * radial)
    text_loss[...] = total[:, width : width + 1] / (WINDOW * 4 * q)


def grad_kernel(parts, embedded_in, grad_out, embedded, grad, sems):
    load = pltpu.make_async_copy(embedded_in, embedded, sems.at[8])
    load.start()
    load.wait()
    rows = grad.shape[0] // 2
    stores = []
    for half in range(2):
        chunk = pl.ds(half * rows, rows)
        grad_sum = (parts[0, chunk, :].astype(f32) + parts[1, chunk, :].astype(f32)) + (
            parts[2, chunk, :].astype(f32) + parts[3, chunk, :].astype(f32)
        )
        inverse, unit_value = unit_rows(embedded[chunk, :])
        radial = jnp.sum(unit_value * grad_sum, axis=-1, keepdims=True)
        grad[chunk, :] = (inverse * (grad_sum - unit_value * radial)).astype(bf16)
        for k in range(4):
            stores.append(
                pltpu.make_async_copy(
                    grad.at[chunk], grad_out.at[k, chunk], sems.at[4 * half + k]
                )
            )
            stores[-1].start()
    for store in stores:
        store.wait()


def pre_kernel(grad_image, w_down, slope_in, grad_pre, slope, sems):
    load = copied(sems, (slope_in, slope))[0]
    grad_act = dot(grad_image[...], w_down[...], 1, 1)
    load.wait()
    grad_pre[...] = (grad_act * slope[...]).astype(bf16)


def up_kernel(info, mine, got, grads, wire_out, wire, sems):
    rows = grads.shape[0] // 2
    core = info[0]
    own = grads[pl.ds(pl.multiple_of(core * rows, rows), rows), :]
    other = grads[pl.ds(pl.multiple_of((1 - core) * rows, rows), rows), :]
    count = mine.shape[0] // 2
    chips = wire.shape[1]
    main = dot(mine[:count, :], own, 1, 0) + dot(got[:count, :], other, 1, 0)
    rest = dot(mine[count:, :], own, 1, 0) + dot(got[count:, :], other, 1, 0)
    place = lax.broadcasted_iota(jnp.int32, (count, LANES), 0) % 8
    blocks = [main[:, k * LANES : (k + 1) * LANES] for k in range(5)]
    ninth = jnp.zeros((count, LANES), f32)
    for k in range(5):
        ninth = jnp.where(place == k, rest[:, k * LANES : (k + 1) * LANES], ninth)
    blocks.append(ninth)
    stores = []
    for k in range(3):
        both = jnp.concatenate(
            [blocks[k].reshape(chips, 8, LANES), blocks[k + 3].reshape(chips, 8, LANES)], axis=1
        )
        wire[k] = both.astype(bf16)
        stores.append(
            pltpu.make_async_copy(
                wire.at[k], wire_out.at[:, :, pl.ds(k * LANES, LANES)], sems.at[k]
            )
        )
        stores[-1].start()
    for store in stores:
        store.wait()


def up_sum_kernel(terms, up_grad):
    total = jnp.sum(terms[...].astype(f32), axis=0)
    up_grad[:8, : 3 * LANES] = total[:8, :]
    up_grad[:8, 3 * LANES :] = total[8:, : 2 * LANES]
    for k in range(5):
        up_grad[8:9, k * LANES : (k + 1) * LANES] = total[8 + k : 9 + k, 2 * LANES :]


def body(pooled, ln_gain, w_up, b_up, w_down, text, logit_scale, logit_bias):
    rows_count, width = pooled.shape
    q = text.shape[0]
    units = w_up.shape[1]
    core = lax.axis_index("c")
    info = jnp.stack([core, lax.axis_index("mp")]).astype(jnp.int32)
    wide = width + LANES

    def mp_exchange(partial):
        return lax.all_to_all(partial.reshape(4, q, width), "mp", 0, 0, tiled=True)

    whole = pltpu.HBM((rows_count, width), bf16)
    copies = pltpu.HBM((4, q, width), bf16)
    sems = pltpu.SemaphoreType.DMA((9,))

    normed, own, partial_out, hidden = call(
        head_kernel,
        (
            pltpu.HBM((rows_count, width), bf16),
            shape((q, width), bf16),
            pltpu.HBM((rows_count, width), bf16),
            pltpu.HBM((rows_count, units), f32),
        ),
        [SMEM] + [HBM] * 5,
        info,
        *(in_hbm(a) for a in (pooled, ln_gain, b_up, w_up, w_down)),
        specs=(HBM, VMEM, HBM, HBM),
        scratch=(
            pltpu.VMEM(pooled.shape, bf16),
            pltpu.VMEM((width,), f32),
            pltpu.VMEM((units,), f32),
            pltpu.VMEM(w_up.shape, bf16),
            pltpu.VMEM(w_down.shape, bf16),
            pltpu.VMEM(pooled.shape, bf16),
            pltpu.VMEM((rows_count, units), f32),
            pltpu.VMEM(pooled.shape, bf16),
            sems,
        ),
    )
    parts = mp_exchange(partial_out)

    text_half = call(text_kernel, shape((q, width), bf16), [VMEM], after(text, partial_out))
    pair = of_both_cores(text_half)
    side_in = moved(pair, [(i, i + 2) if i % 2 == 0 else (i, i - 2) for i in range(N_DP)])
    far_out = [(i - 3, i) if i % 2 == 0 else (i + 3, i) for i in range(N_DP)]
    far = moved(text_half, far_out)

    half_rows = shape((1024, rows_count), bf16)
    mine, theirs, slope = call(
        select_kernel,
        (half_rows, half_rows, pltpu.HBM((rows_count, units), f32)),
        [SMEM, VMEM, VMEM],
        info,
        normed,
        hidden,
        specs=(VMEM, VMEM, HBM),
        scratch=(pltpu.VMEM((rows_count, units), f32), sems),
    )

    embedded, image_half = call(
        embed_kernel,
        (pltpu.HBM((q, width), f32), copies),
        [VMEM, VMEM],
        parts,
        after(own, theirs, pair, far),
        specs=(HBM, HBM),
        scratch=(pltpu.VMEM((q, width), bf16), pltpu.VMEM((q, width), f32), sems),
    )
    unit_half = mp_exchange(image_half).reshape(rows_count, width)

    sides = of_both_cores(after(side_in, image_half))
    texts = call(
        window_kernel,
        shape((WINDOW * q, width), bf16),
        [VMEM] * 4,
        sides[: 2 * q],
        pair,
        sides[2 * q :],
        far,
    )


    image_part = call(
        image_kernel,
        whole,
        [SMEM] * 3 + [VMEM] * 2,
        info,
        logit_scale,
        logit_bias,
        unit_half,
        texts,
        specs=HBM,
        scratch=(pltpu.VMEM((rows_count, width), bf16), sems),
    )
    grad_parts = mp_exchange(image_part)
    got_rows = swapped(after(theirs, image_part))

    give, far_part, keep_side, keep_own = call(
        text_part_kernel,
        (
            shape((3 * q, wide), bf16),
            shape((q, wide), bf16),
            shape((2 * q, wide), f32),
            shape((q, wide), f32),
        ),
        [SMEM] * 3 + [VMEM] * 2,
        info,
        logit_scale,
        logit_bias,
        after(unit_half, image_part),
        texts,
    )
    far_back = moved(after(far_part, grad_parts), [(d, s) for s, d in far_out])
    side, own_sum = call(
        side_kernel,
        (shape((2 * q, wide), bf16), shape((q, wide), f32)),
        [SMEM] + [VMEM] * 3,
        info,
        of_both_cores(give),
        keep_side,
        keep_own,
    )

    grad_own = call(
        grad_kernel,
        copies,
        [VMEM, HBM],
        after(grad_parts, side),
        in_hbm(embedded),
        specs=HBM,
        scratch=(pltpu.VMEM((q, width), f32), pltpu.VMEM((q, width), bf16), sems),
    )
    grad_image = mp_exchange(grad_own).reshape(rows_count, width)
    side = after(side, grad_own)
    came = moved(side, [(i, i - 2) if i % 2 == 0 else (i, i + 2) for i in range(N_DP)])

    grad_pre = call(
        pre_kernel,
        shape((rows_count, units), bf16),
        [VMEM, VMEM, HBM],
        grad_image,
        w_down,
        in_hbm(slope),
        scratch=(pltpu.VMEM((rows_count, units), f32), sems),
    )
    grads = of_both_cores(grad_pre)
    up_wire = call(
        up_kernel,
        pltpu.HBM((N_DP // 2, 16, 3 * LANES), bf16),
        [SMEM] + [VMEM] * 3,
        info,
        mine,
        got_rows,
        after(grads, came, far_back),
        specs=HBM,
        scratch=(pltpu.VMEM((3, N_DP // 2, 16, LANES), bf16), sems),
    )
    up_terms = lax.all_to_all(up_wire, CHIPS, 0, 0, tiled=True)

    text_grad, text_loss = call(
        text_grad_kernel,
        (shape((q, width), f32), shape((q, 1), f32)),
        [SMEM] + [VMEM] * 4,
        info,
        of_both_cores(after(came, up_wire)),
        own_sum,
        far_back,
        text,
    )
    text_loss = text_loss.reshape(q)

    up_grad = call(up_sum_kernel, shape((width // N_DP, units), f32), [VMEM], up_terms)
    return (up_grad, text_grad, text_loss)


def solution(mesh):
    fine = Mesh(mesh.devices.reshape(4, 2, 8, 2, 4), ("x", "zl", "y", "c", "mp"))
    every = (*DP, "mp")
    placed = (
        P(DP, None),
        P(),
        P(None, "mp"),
        P("mp"),
        P("mp", None),
        P(every, None),
        P(),
        P(),
    )
    return jax.shard_map(
        body,
        mesh=fine,
        in_specs=placed,
        out_specs=(P(DP, "mp"), P(every, None), P(every)),
        check_vma=False,
    )
```
